32 devices in a mesh: groups: 2 (over y), layer: 4 (over x, core), tok: 4 (over z).
Axes of the slice: x: 2, y: 2, z: 4, core: 2. Of those that a mesh axis runs over, the one named last changes fastest.
Arguments:
- keys: bfloat16 [4, 8192, 1024], P('layer', ('groups', 'tok')), parts along dimension 1, may hold values from -6 to 6
Outputs:
- gram_tiles: float32 [4, 3, 2048, 1024], P('layer', None, ('groups', 'tok')), parts along dimension 2
The draws below stay inside these ranges and needn't reach their ends.
There are 2 independent parts, one for each index of `groups`. The reference program is written for one: setup_inputs(seed, part) draws one part's arguments, and reference() takes and returns one part's arrays. A program takes and returns all parts, laid end to end along the dimension named above; each array names one. Nothing has to cross between parts.
All inputs are finite; a program needn't handle non-finite values.
Results may differ from the reference program's by a relative error of at most 0.0003.
Values may be sent and summed in bfloat16 or wider, within the bound.
No kernel may reach another device: no remote copies, remote signals or barrier semaphores. Data moves between devices by JAX's collectives and lax.ppermute only.
A program may use at most 64 MiB of HBM per device.

```python
import jax
import jax.numpy as jnp
from jax import lax

TOK_DEV = 1024
KEY_WIDTH = 1024
LAYERS = 4
SPANS = 3
TOKENS = 4096
N_TOK = 4


def levels(stream_key, dims, shards, smallest, largest):
    loudness, own = 1.0, jax.random.fold_in(stream_key, 6)
    for axis_at, blocks in shards:
        steps = jnp.exp(jax.random.uniform(jax.random.fold_in(own, axis_at), (blocks,), jnp.float32, smallest / len(shards), largest / len(shards)))
        loudness = loudness * jnp.repeat(steps, dims[axis_at] // blocks).reshape([-1 if axis == axis_at else 1 for axis in range(len(dims))])
    return loudness


def noise(rng, shape, deviation, bound, shards=(), held_as=jnp.bfloat16):
    array = jax.random.normal(rng, shape, jnp.float32) * deviation
    if len(shards) > 0:
        array = levels(rng, shape, shards, -0.22, 0.18) * array
    return jnp.clip(array, min=-bound, max=bound).astype(held_as)


def setup_inputs(seed: int = 0, part: int = 0) -> dict:
    seeds = jax.random.split(jax.random.key(seed), 2)
    part_splits = jax.random.split(jax.random.fold_in(seeds[1], part), 2)
    return {
        "keys": noise(part_splits[0], (LAYERS, TOKENS, KEY_WIDTH), 1.0, 6.0, ((0, 4), (1, 4))),
    }


def shard_partials(first_keys, second_keys):
    first_blocks = first_keys.reshape(N_TOK, TOK_DEV, KEY_WIDTH).astype(jnp.float32)
    second_blocks = second_keys.reshape(N_TOK, TOK_DEV, KEY_WIDTH).astype(jnp.float32)
    partial_sums = jnp.einsum('ste,stf->sef', first_blocks, second_blocks) * (1.0 / TOKENS)
    return jnp.sum(partial_sums, axis=0)


def reference(keys):
    def one_pair(pair_index):
        layer_index = pair_index // SPANS
        distance = pair_index % SPANS
        other_index = (layer_index + distance) % LAYERS
        first_keys = lax.dynamic_index_in_dim(keys, layer_index, 0, keepdims=False)
        second_keys = lax.dynamic_index_in_dim(keys, other_index, 0, keepdims=False)
        return shard_partials(first_keys, second_keys)

    tiles = lax.map(one_pair, jnp.arange(LAYERS * SPANS, dtype=jnp.int32))
    return tiles.reshape(LAYERS, SPANS, KEY_WIDTH, KEY_WIDTH)
```

```python
import functools

import jax
import jax.numpy as jnp
from jax import lax
from jax.experimental import pallas as pl
from jax.experimental.pallas import tpu as pltpu
from jax.sharding import PartitionSpec as P

OUTER_TO_INNER = [(0, 1), (3, 2)]
ACROSS_MIDDLE = [(1, 2), (2, 1)]
INNER_TO_OUTER = [(1, 0), (2, 3)]
FAR, NEXT, NEAR = 3, 2, 1

HALF = 128
TAIL = 16
SPREAD = 13777.0
SMALLEST = 1e-30
COST = 10_000_000_000
VMEM_BYTES = 24 * 1024 * 1024


def shifted(value, axis, steps):
    count = lax.axis_size(axis)
    pairs = [(source, (source + steps) % count) for source in range(count)]
    return lax.ppermute(value, axis, pairs)


def tile_rows(inverse, left_keys, right_keys):
    product = lax.dot_general(
        left_keys, right_keys, (((0,), (0,)), ((), ())), preferred_element_type=jnp.float32
    )
    return product * inverse


def reduce_scattered(own_keys, forward_list, inverse):
    shares = [
        lax.psum_scatter(
            tile_rows(inverse, own_keys, right_keys), "tok", scatter_dimension=0, tiled=True
        )
        for right_keys in forward_list
    ]
    return jnp.stack(shares)[None]


def fold():
    place = lax.axis_index("tok")
    upper = place >= 2
    inner = jnp.logical_or(place == 1, place == 2)
    return upper, inner


def block_at(upper, index):
    return jnp.where(upper, 3 - index, index)


def product(inverse, left_ref, right_ref, upper, row, column, rows):
    left = left_ref[:, pl.ds(pl.multiple_of(block_at(upper, row) * rows, rows), rows)]
    if column is None:
        return tile_rows(inverse, left, right_ref[...])
    at = pl.ds(pl.multiple_of(block_at(upper, column) * rows, rows), rows)
    return tile_rows(inverse, left, right_ref[:, at])


def row_factor(rows):
    index = lax.broadcasted_iota(jnp.int32, (rows, HALF), 0).astype(jnp.float32) * 0.6180339887
    return 1.0 + (index - jnp.floor(index))


def column_factor(half):
    index = lax.broadcasted_iota(jnp.int32, (1, HALF), 1).astype(jnp.float32) + float(half * HALF)
    index = index * 0.7548776662
    return 1.0 + (index - jnp.floor(index))


def peak_of(value):
    return jnp.max(jnp.max(jnp.abs(value), axis=0, keepdims=True), axis=1, keepdims=True)


def write_message(message_ref, blocks):
    rows = blocks[0].shape[0]
    peak = functools.reduce(jnp.maximum, [peak_of(block) for block in blocks])
    peak = (jnp.maximum(peak, SMALLEST) * 1.02).astype(jnp.bfloat16).astype(jnp.float32)
    peak = jnp.broadcast_to(peak, (1, HALF))
    factor = row_factor(rows)
    for number, block in enumerate(blocks):
        for half in range(rows // HALF):
            scaled = block[:, half * HALF : (half + 1) * HALF] * factor
            scaled = scaled * (column_factor(half) * (SPREAD / peak))
            power = scaled * scaled
            power = power * power
            power = power * power
            coded = jnp.where(scaled < 0.0, -power, power)
            start = (number * (rows // HALF) + half) * rows
            message_ref[start : start + rows, :] = coded.astype(jnp.bfloat16)
    start = len(blocks) * (rows // HALF) * rows
    message_ref[start : start + TAIL, :] = jnp.broadcast_to(peak, (TAIL, HALF)).astype(jnp.bfloat16)


def read_block(message_ref, number, rows):
    peak = message_ref[message_ref.shape[0] - TAIL :, :].astype(jnp.float32)[0:1]
    factor = 1.0 / row_factor(rows)
    halves = []
    for half in range(rows // HALF):
        start = (number * (rows // HALF) + half) * rows
        coded = message_ref[start : start + rows, :].astype(jnp.float32)
        root = lax.rsqrt(lax.rsqrt(jnp.maximum(jnp.abs(coded), 1.2e-38)))
        root = root * lax.rsqrt(root)
        root = jnp.where(coded < 0.0, -root, root)
        halves.append(root * factor * (peak * (1.0 / SPREAD) / column_factor(half)))
    return jnp.concatenate(halves, axis=1)


def message_shape(count, rows):
    return jax.ShapeDtypeStruct((count * rows * rows // HALF + TAIL, HALF), jnp.bfloat16)


def columns_of(value, upper_value, rows, index):
    return jnp.where(
        upper_value,
        value[:, (3 - index) * rows : (4 - index) * rows],
        value[:, index * rows : (index + 1) * rows],
    )


def send_kernel(parts, inverse, left_ref, *refs):
    *right_refs, message_ref = refs
    rows = left_ref.shape[1] // 4
    upper, inner = fold()

    @pl.when(jnp.logical_not(inner))
    def _():
        write_message(
            message_ref,
            [
                product(inverse, left_ref, right_refs[which], upper, row, column, rows)
                for which, row, count in parts
                for column in range(count)
            ],
        )


def pass_on_kernel(parts, inverse, left_ref, right_ref, message_ref, copy_ref):
    copy_ref[...] = right_ref[...]
    send_kernel(parts, inverse, left_ref, right_ref, message_ref)


def copy_block(turned_ref, message_ref, number, rows):
    size = rows * rows // HALF
    turned_ref[0:size, :] = message_ref[number * size : (number + 1) * size, :]
    turned_ref[size : size + TAIL, :] = message_ref[message_ref.shape[0] - TAIL :, :]


def cross_kernel(row, count, inverse, left_ref, right_ref, in_ref, message_ref, *turned_refs):
    rows = left_ref.shape[1] // 4
    upper, inner = fold()

    @pl.when(inner)
    def _():
        write_message(
            message_ref,
            [
                product(inverse, left_ref, right_ref, upper, row, column, rows)
                + read_block(in_ref, column, rows)
                for column in range(count)
            ],
        )
        for turned_ref in turned_refs:
            copy_block(turned_ref, in_ref, 1, rows)


def back_kernel(inverse, left_ref, right_ref, across_ref, message_ref, *turned_refs):
    rows = left_ref.shape[1] // 4
    upper, inner = fold()

    @pl.when(inner)
    def _():
        write_message(
            message_ref,
            [
                product(inverse, left_ref, right_ref, upper, 0, column, rows)
                + read_block(across_ref, 3 - column, rows)
                for column in range(4)
            ],
        )
        for turned_ref in turned_refs:
            copy_block(turned_ref, across_ref, 2, rows)


def put(out_ref, upper, column, rows, value):
    at = pl.ds(pl.multiple_of(block_at(upper, column) * rows, rows), rows)
    out_ref[0, 0, :, at] = value


def finish_kernel(near_at, turned_at, inverse, left_ref, right_ref, near_ref, next_ref, back_ref, *refs):
    *turned_refs, token_ref, out_ref = refs
    token_ref[...] = jnp.zeros_like(token_ref)
    folds = len(turned_at) > 0
    rows = left_ref.shape[1] // 4
    upper, inner = fold()

    @pl.when(jnp.logical_not(inner))
    def _():
        for column in range(4):
            own = product(inverse, left_ref, right_ref, upper, 0, column, rows)
            put(out_ref, upper, column, rows, own + read_block(back_ref, column, rows))

    def turned_block(number):
        return read_block(turned_refs[number], turned_at[number], rows).T

    @pl.when(inner)
    def _():
        for column in range(4):
            own = product(inverse, left_ref, right_ref, upper, 1, column, rows)
            if folds and column >= 2:
                own = own + turned_block(3 - column)
            else:
                own = own + read_block(near_ref, near_at + column, rows)
            if folds and column == 0:
                own = own + turned_block(2)
            else:
                own = own + read_block(next_ref, 3 - column, rows)
            put(out_ref, upper, column, rows, own)


def ordered(body, count, held, *refs):
    body(*refs[:count], *refs[count + held :])


def call(body, operands, held, cost, out_shape, **options):
    specs = [pl.BlockSpec(memory_space=pltpu.VMEM)] * len(operands)
    specs += [pl.BlockSpec(memory_space=pl.ANY)] * len(held)
    return pl.pallas_call(
        functools.partial(ordered, body, len(operands), len(held)),
        out_shape=out_shape,
        in_specs=specs,
        compiler_params=pltpu.CompilerParams(vmem_limit_bytes=VMEM_BYTES),
        cost_estimate=pl.CostEstimate(flops=cost, bytes_accessed=cost // 1000, transcendentals=0),
        **options,
    )(*operands, *held)


def folded_line(own_keys, inverse):
    width = own_keys.shape[1]
    rows = width // 4
    last = [own_keys]

    def run(body, operands, shapes, held=(), **options):
        held = (*held, last[0])
        result = call(functools.partial(body, inverse), operands, held, COST, shapes, **options)
        last[0] = jax.tree.leaves(result)[0]
        return result

    def send(rights, *parts):
        count = sum(part[-1] for part in parts)
        operands = (own_keys, *rights)
        message = run(functools.partial(send_kernel, parts), operands, message_shape(count, rows))
        return lax.ppermute(message, "tok", OUTER_TO_INNER)

    def swap(messages):
        half_turn = [(source, (source + 2) % 4) for source in range(4)]
        return [lax.ppermute(message, "layer", half_turn) for message in messages]

    def cross(right, row, count, arrived, swaps=0):
        body = functools.partial(cross_kernel, row, count)
        shapes = [message_shape(count, rows)] + [message_shape(1, rows)] * swaps
        message, *turned = run(body, (own_keys, right, arrived), shapes)
        return lax.ppermute(message, "tok", ACROSS_MIDDLE), *swap(turned)

    def back(right, crossed, swaps=0):
        shapes = [message_shape(4, rows)] + [message_shape(1, rows)] * swaps
        message, *turned = run(back_kernel, (own_keys, right, crossed), shapes)
        return lax.ppermute(message, "tok", INNER_TO_OUTER), *swap(turned)

    def finish(out, distance, right, near_at, turned_at, *operands):
        options = {}
        operands = (own_keys, right, *operands)
        if out is not None:
            options = {"held": (out,), "input_output_aliases": {len(operands): 1}}
        token, out = run(
            functools.partial(finish_kernel, near_at, turned_at),
            operands,
            [
                jax.ShapeDtypeStruct((TAIL, HALF), jnp.bfloat16),
                jax.ShapeDtypeStruct((1, 3, rows, width), jnp.float32),
            ],
            grid=(1,),
            out_specs=[
                pl.BlockSpec((TAIL, HALF), lambda step: (0, 0)),
                pl.BlockSpec((1, 1, rows, width), lambda step: (0, distance, 0, 0)),
            ],
            **options,
        )
        return out

    second_keys = shifted(own_keys, "layer", -1)
    far_0 = send((own_keys,), (0, FAR, 4))
    rest_0 = send((own_keys,), (0, NEXT, 3), (0, NEAR, 2))
    (far_across_0,) = cross(own_keys, FAR, 4, far_0)
    far_1, passed = run(
        functools.partial(pass_on_kernel, ((0, FAR, 4),)),
        (own_keys, second_keys),
        [message_shape(4, rows), jax.ShapeDtypeStruct(own_keys.shape, own_keys.dtype)],
    )
    third_keys = shifted(passed, "layer", -1)
    far_1 = lax.ppermute(far_1, "tok", OUTER_TO_INNER)
    next_1 = send((second_keys,), (0, NEXT, 4))
    (next_across_0,) = cross(own_keys, NEXT, 3, rest_0)
    (back_0,) = back(own_keys, far_across_0)
    (far_across_1,) = cross(second_keys, FAR, 4, far_1)
    far_2 = send((third_keys,), (0, FAR, 4))
    next_2 = send((third_keys,), (0, NEXT, 3))
    (next_across_1,) = cross(second_keys, NEXT, 4, next_1)
    (back_1,) = back(second_keys, far_across_1)
    out = finish(
        None, 0, own_keys, 3, (1, 1, 2), rest_0, next_across_0, back_0, far_0, rest_0, far_across_0
    )
    near = send((second_keys, third_keys), (0, NEAR, 4), (1, NEAR, 2))
    far_across_2, turned_far = cross(third_keys, FAR, 4, far_2, 1)
    next_across_2, turned_next = cross(third_keys, NEXT, 3, next_2, 1)
    back_2, turned_across = back(third_keys, far_across_2, 1)
    out = finish(out, 1, second_keys, 0, (), near, next_across_1, back_1)
    turned = (turned_far, turned_next, turned_across)
    return finish(out, 2, third_keys, 4, (0, 0, 0), near, next_across_2, back_2, *turned)


def per_device(keys):
    own_keys = keys[0]
    layers = lax.axis_size("layer")
    half_span = layers // 2
    inverse = 1.0 / (own_keys.shape[0] * lax.axis_size("tok"))
    if lax.axis_size("tok") == 4 and layers == 4 and own_keys.shape[1] % (8 * HALF) == 0:
        return folded_line(own_keys, inverse)
    forward_list = [own_keys]
    for repeat in range(half_span):
        forward_list.append(shifted(forward_list[-1], "layer", -1))
    return reduce_scattered(own_keys, forward_list, inverse)


def solution(mesh):
    in_specs = (P("layer", ("groups", "tok"), None),)
    out_specs = P("layer", None, ("groups", "tok"), None)
    return jax.shard_map(
        per_device, mesh=mesh, in_specs=in_specs, out_specs=out_specs, check_vma=False
    )
```

```python
import functools

import jax
import jax.numpy as jnp
from jax import lax
from jax.experimental import pallas as pl
from jax.experimental.pallas import tpu as pltpu
from jax.sharding import PartitionSpec as P

OUTER_TO_INNER = [(0, 1), (3, 2)]
ACROSS_MIDDLE = [(1, 2), (2, 1)]
INNER_TO_OUTER = [(1, 0), (2, 3)]
FAR, NEXT, NEAR = 3, 2, 1

HALF = 128
TAIL = 16
SPREAD = 13777.0
SMALLEST = 1e-30
COSTS = tuple(1_000_000_000 * cost for cost in (3, 3, 3, 30, 4, 4, 4, 4, 4, 4, 4, 4, 4, 4, 4, 4, 4, 4, 4, 4, 4))
VMEM_BYTES = 24 * 1024 * 1024


def shifted(value, axis, steps):
    count = lax.axis_size(axis)
    pairs = [(source, (source + steps) % count) for source in range(count)]
    return lax.ppermute(value, axis, pairs)


def tile_rows(inverse, left_keys, right_keys):
    product = lax.dot_general(
        left_keys, right_keys, (((0,), (0,)), ((), ())), preferred_element_type=jnp.float32
    )
    return product * inverse


def reduce_scattered(own_keys, forward_list, inverse):
    shares = [
        lax.psum_scatter(
            tile_rows(inverse, own_keys, right_keys), "tok", scatter_dimension=0, tiled=True
        )
        for right_keys in forward_list
    ]
    return jnp.stack(shares)[None]


def fold():
    place = lax.axis_index("tok")
    upper = place >= 2
    inner = jnp.logical_or(place == 1, place == 2)
    return upper, inner


def block_at(upper, index):
    return jnp.where(upper, 3 - index, index)


def product(inverse, left_ref, right_ref, upper, row, column, rows):
    left = left_ref[:, pl.ds(pl.multiple_of(block_at(upper, row) * rows, rows), rows)]
    if column is None:
        return tile_rows(inverse, left, right_ref[...])
    at = pl.ds(pl.multiple_of(block_at(upper, column) * rows, rows), rows)
    return tile_rows(inverse, left, right_ref[:, at])


def row_factor(rows):
    index = lax.broadcasted_iota(jnp.int32, (rows, HALF), 0).astype(jnp.float32) * 0.6180339887
    return 1.0 + (index - jnp.floor(index))


def column_factor(half):
    index = lax.broadcasted_iota(jnp.int32, (1, HALF), 1).astype(jnp.float32) + float(half * HALF)
    index = index * 0.7548776662
    return 1.0 + (index - jnp.floor(index))


def peak_of(value):
    return jnp.max(jnp.max(jnp.abs(value), axis=0, keepdims=True), axis=1, keepdims=True)


def code(scaled):
    power = scaled * scaled
    power = power * power
    power = power * power
    return jnp.where(scaled < 0.0, -power, power)


def decoded(coded):
    root = lax.rsqrt(lax.rsqrt(jnp.maximum(jnp.abs(coded), 1.2e-38)))
    root = root * lax.rsqrt(root)
    return jnp.where(coded < 0.0, -root, root)


def write_message(message_ref, blocks, diagonal=None):
    rows = blocks[0].shape[0]
    peak = functools.reduce(jnp.maximum, [peak_of(block) for block in blocks])
    peak = (jnp.maximum(peak, SMALLEST) * 1.02).astype(jnp.bfloat16).astype(jnp.float32)
    peak = jnp.broadcast_to(peak, (1, HALF))
    factor = row_factor(rows)
    for number, block in enumerate(blocks):
        for half in range(rows // HALF):
            scaled = block[:, half * HALF : (half + 1) * HALF] * factor
            scaled = scaled * (column_factor(half) * (SPREAD / peak))
            start = (number * (rows // HALF) + half) * rows
            message_ref[start : start + rows, :] = code(scaled).astype(jnp.bfloat16)
    start = len(blocks) * (rows // HALF) * rows
    if diagonal is not None:
        write_diagonal(message_ref, start, diagonal, peak)
        start += rows // HALF * TAIL
    message_ref[start : start + TAIL, :] = jnp.broadcast_to(peak, (TAIL, HALF)).astype(jnp.bfloat16)


def place_in_block(rows):
    row = lax.broadcasted_iota(jnp.int32, (rows, rows), 0)
    return row, lax.broadcasted_iota(jnp.int32, (rows, rows), 1)


def write_diagonal(message_ref, start, block, peak):
    rows = block.shape[0]
    row, column = place_in_block(rows)
    line = jnp.sum(jnp.where(row == column, block, 0.0), axis=0, keepdims=True)
    for half in range(rows // HALF):
        scaled = line[:, half * HALF : (half + 1) * HALF] * (column_factor(half) * (SPREAD / peak))
        coded = jnp.broadcast_to(code(scaled), (TAIL, HALF))
        message_ref[start + half * TAIL : start + (half + 1) * TAIL, :] = coded.astype(jnp.bfloat16)


def read_packed(message_ref, number, rows):
    packed = read_block(message_ref, number, rows)
    peak = message_ref[message_ref.shape[0] - TAIL :, :].astype(jnp.float32)[0:1]
    start = message_ref.shape[0] - TAIL - rows // HALF * TAIL
    line = []
    for half in range(rows // HALF):
        coded = message_ref[start + half * TAIL : start + (half + 1) * TAIL, :].astype(jnp.float32)
        line.append(decoded(coded[0:1]) * (peak * (1.0 / SPREAD) / column_factor(half)))
    line = jnp.broadcast_to(jnp.concatenate(line, axis=1), (rows, rows))
    row, column = place_in_block(rows)
    return jnp.where(row < column, packed, jnp.where(row == column, line, packed.T))


def read_block(message_ref, number, rows):
    peak = message_ref[message_ref.shape[0] - TAIL :, :].astype(jnp.float32)[0:1]
    factor = 1.0 / row_factor(rows)
    halves = []
    for half in range(rows // HALF):
        start = (number * (rows // HALF) + half) * rows
        coded = message_ref[start : start + rows, :].astype(jnp.float32)
        factors = peak * (1.0 / SPREAD) / column_factor(half)
        halves.append(decoded(coded) * factor * factors)
    return jnp.concatenate(halves, axis=1)


def message_shape(count, rows, diagonals=0):
    tails = TAIL + diagonals * rows // HALF * TAIL
    return jax.ShapeDtypeStruct((count * rows * rows // HALF + tails, HALF), jnp.bfloat16)


def columns_of(value, upper_value, rows, index):
    return jnp.where(
        upper_value,
        value[:, (3 - index) * rows : (4 - index) * rows],
        value[:, index * rows : (index + 1) * rows],
    )


def send_kernel(parts, inverse, left_ref, *refs):
    *right_refs, message_ref = refs
    rows = left_ref.shape[1] // 4
    upper, inner = fold()

    @pl.when(jnp.logical_not(inner))
    def _():
        write_message(
            message_ref,
            [
                product(inverse, left_ref, right_refs[which], upper, row, column, rows)
                for which, row, count in parts
                for column in range(count)
            ],
        )


def rest_kernel(inverse, left_ref, right_ref, message_ref):
    rows = left_ref.shape[1] // 4
    upper, inner = fold()

    @pl.when(jnp.logical_not(inner))
    def _():
        def own(row, column):
            return product(inverse, left_ref, right_ref, upper, row, column, rows)

        row, column = place_in_block(rows)
        near = own(NEAR, NEAR)
        packed = jnp.where(row >= column, own(NEXT, NEXT), near)
        write_message(message_ref, [own(NEXT, 0), own(NEXT, 1), packed, own(NEAR, 0)], near)


def copy_block(turned_ref, message_ref, number, rows):
    size = rows * rows // HALF
    turned_ref[0:size, :] = message_ref[number * size : (number + 1) * size, :]
    turned_ref[size : size + TAIL, :] = message_ref[message_ref.shape[0] - TAIL :, :]


def cross_kernel(row, columns, inverse, left_ref, right_ref, in_ref, message_ref):
    rows = left_ref.shape[1] // 4
    upper, inner = fold()

    @pl.when(inner)
    def _():
        write_message(
            message_ref,
            [
                product(inverse, left_ref, right_ref, upper, row, column, rows)
                + read_block(in_ref, column, rows)
                for column in columns
            ],
        )


def back_kernel(columns, inverse, left_ref, right_ref, across_ref, *refs):
    message_ref = refs[0] if len(refs) == 1 else refs[2]
    rows = left_ref.shape[1] // 4
    size = rows * rows // HALF + TAIL
    upper, inner = fold()

    @pl.when(inner)
    def _():
        write_message(
            message_ref,
            [
                product(inverse, left_ref, right_ref, upper, 0, 3 - column, rows)
                + read_block(across_ref, number, rows)
                for number, column in enumerate(columns)
            ],
        )
        if len(refs) > 1:
            far_ref, next_ref, _, turned_ref = refs
            copy_block(turned_ref.at[pl.ds(0, size)], far_ref, 1, rows)
            copy_block(turned_ref.at[pl.ds(size, size)], next_ref, 1, rows)
            copy_block(turned_ref.at[pl.ds(2 * size, size)], across_ref, columns.index(2), rows)


def put(out_ref, upper, column, rows, value):
    at = pl.ds(pl.multiple_of(block_at(upper, column) * rows, rows), rows)
    out_ref[0, 0, :, at] = value


def finish_kernel(near_at, turned_at, packs, backs, inverse, left_ref, right_ref, next_ref, near_ref, *refs):
    *refs, token_ref, out_ref = refs
    back_refs, turned_refs = refs[: len(backs)], refs[len(backs) :]
    token_ref[...] = jnp.zeros_like(token_ref)
    folds = len(turned_at) > 0
    rows = left_ref.shape[1] // 4
    upper, inner = fold()

    @pl.when(jnp.logical_not(inner))
    def _():
        for back_ref, columns in zip(back_refs, backs):
            for number, column in enumerate(columns):
                own = product(inverse, left_ref, right_ref, upper, 0, 3 - column, rows)
                put(out_ref, upper, 3 - column, rows, own + read_block(back_ref, number, rows))

    def turned_block(number):
        if len(turned_refs) == 1:
            size = rows * rows // HALF + TAIL
            return read_block(turned_refs[0].at[pl.ds(number * size, size)], 0, rows).T
        return read_block(turned_refs[number], turned_at[number], rows).T

    @pl.when(inner)
    def _():
        for column in range(4):
            own = product(inverse, left_ref, right_ref, upper, 1, column, rows)
            if folds and column >= 2:
                own = own + turned_block(3 - column)
            elif packs and column == 1:
                own = own + read_packed(near_ref, 2, rows)
            else:
                own = own + read_block(near_ref, near_at + column, rows)
            if folds and column == 0:
                own = own + turned_block(2)
            elif packs and column == 1:
                across = read_block(next_ref, 2, rows)
                row, place = place_in_block(rows)
                own = own + jnp.where(row >= place, across, across.T)
            else:
                own = own + read_block(next_ref, 3 - column, rows)
            put(out_ref, upper, column, rows, own)


def ordered(body, count, held, *refs):
    body(*refs[:count], *refs[count + held :])


def call(body, operands, held, cost, out_shape, **options):
    specs = [pl.BlockSpec(memory_space=pltpu.VMEM)] * len(operands)
    specs += [pl.BlockSpec(memory_space=pl.ANY)] * len(held)
    return pl.pallas_call(
        functools.partial(ordered, body, len(operands), len(held)),
        out_shape=out_shape,
        in_specs=specs,
        compiler_params=pltpu.CompilerParams(vmem_limit_bytes=VMEM_BYTES),
        cost_estimate=pl.CostEstimate(flops=cost, bytes_accessed=cost // 1000, transcendentals=0),
        **options,
    )(*operands, *held)


def folded_line(own_keys, inverse):
    width = own_keys.shape[1]
    rows = width // 4
    last, calls = [own_keys], []

    def run(body, operands, shapes, held=(), **options):
        held = (*held, last[0])
        cost = int(COSTS[len(calls)])
        calls.append(cost)
        result = call(functools.partial(body, inverse), operands, held, cost, shapes, **options)
        last[0] = jax.tree.leaves(result)[0]
        return result

    def send(rights, *parts):
        count = sum(part[-1] for part in parts)
        operands = (own_keys, *rights)
        message = run(functools.partial(send_kernel, parts), operands, message_shape(count, rows))
        return lax.ppermute(message, "tok", OUTER_TO_INNER)

    def cross(right, row, columns, arrived, held=()):
        body = functools.partial(cross_kernel, row, columns)
        message = run(body, (own_keys, right, arrived), message_shape(len(columns), rows), held)
        return lax.ppermute(message, "tok", ACROSS_MIDDLE)

    def back(right, columns, crossed, *arrived, held=()):
        body = functools.partial(back_kernel, columns)
        shapes = [message_shape(len(columns), rows)]
        if arrived:
            block = message_shape(1, rows)
            shapes.append(jax.ShapeDtypeStruct((3 * block.shape[0], HALF), block.dtype))
        message, *turned = run(body, (own_keys, right, crossed, *arrived), shapes, held)
        half_turn = [(source, (source + 2) % 4) for source in range(4)]
        turned = [lax.ppermute(part, "layer", half_turn) for part in turned]
        return lax.ppermute(message, "tok", INNER_TO_OUTER), *turned

    tile = jax.ShapeDtypeStruct((1, 3, rows, width), jnp.float32)
    token = jax.ShapeDtypeStruct((TAIL, HALF), jnp.bfloat16)

    def tile_specs(distance):
        return [
            pl.BlockSpec((TAIL, HALF), lambda step: (0, 0)),
            pl.BlockSpec((1, 1, rows, width), lambda step: (0, distance, 0, 0)),
        ]

    def finish(out, distance, right, next_across, backs, near, turned=(), near_at=0, turned_at=(), packs=False):
        operands = (own_keys, right, next_across, near, *backs.values(), *turned)
        options = {}
        if out is not None:
            options = {"held": (out,), "input_output_aliases": {len(operands): 1}}
        body = functools.partial(finish_kernel, near_at, turned_at, packs, tuple(backs))
        _, out = run(body, operands, [token, tile], grid=(1,), out_specs=tile_specs(distance), **options)
        return out

    every, upper_half, lower_half = (0, 1, 2, 3), (2, 3), (0, 1)
    second_keys = shifted(own_keys, "layer", -1)
    third_keys = shifted(second_keys, "layer", -1)
    far_0 = send((own_keys,), (0, FAR, 4))
    rest_0 = run(rest_kernel, (own_keys, own_keys), message_shape(4, rows, 1))
    rest_0 = lax.ppermute(rest_0, "tok", OUTER_TO_INNER)
    far_across_0 = cross(own_keys, FAR, every, far_0)
    far_1 = send((second_keys,), (0, FAR, 4))
    next_across_0 = cross(own_keys, NEXT, (0, 1, 2), rest_0)
    (back_0,) = back(own_keys, every, far_across_0)
    next_1 = send((second_keys,), (0, NEXT, 4))
    far_across_1 = cross(second_keys, FAR, every, far_1)
    far_2 = send((third_keys,), (0, FAR, 4))
    turned = (far_0, rest_0, far_across_0)
    out = finish(None, 0, own_keys, next_across_0, {every: back_0}, rest_0, turned, 3, (1, 1, 2), True)
    next_across_1 = cross(second_keys, NEXT, every, next_1)
    next_2 = send((third_keys,), (0, NEXT, 3))
    (back_1,) = back(second_keys, every, far_across_1)
    near = send((second_keys, third_keys), (0, NEAR, 4), (1, NEAR, 2))
    far_across_2 = cross(third_keys, FAR, upper_half, far_2)
    far_across_3 = cross(third_keys, FAR, lower_half, far_2, (next_across_1,))
    back_2, turned = back(third_keys, upper_half, far_across_2, far_2, next_2, held=(back_1,))
    next_across_2 = cross(third_keys, NEXT, (0, 1, 2), next_2)
    (back_3,) = back(third_keys, lower_half, far_across_3)
    backs = {upper_half: back_2, lower_half: back_3}
    out = finish(out, 1, second_keys, next_across_1, {every: back_1}, near)
    return finish(out, 2, third_keys, next_across_2, backs, near, (turned,), 4, (0, 0, 0))


def per_device(keys):
    own_keys = keys[0]
    layers = lax.axis_size("layer")
    half_span = layers // 2
    inverse = 1.0 / (own_keys.shape[0] * lax.axis_size("tok"))
    if lax.axis_size("tok") == 4 and layers == 4 and own_keys.shape[1] % (8 * HALF) == 0:
        return folded_line(own_keys, inverse)
    forward_list = [own_keys]
    for repeat in range(half_span):
        forward_list.append(shifted(forward_list[-1], "layer", -1))
    return reduce_scattered(own_keys, forward_list, inverse)


def solution(mesh):
    in_specs = (P("layer", ("groups", "tok"), None),)
    out_specs = P("layer", None, ("groups", "tok"), None)
    return jax.shard_map(
        per_device, mesh=mesh, in_specs=in_specs, out_specs=out_specs, check_vma=False
    )
```

```python
import functools

import jax
import jax.numpy as jnp
from jax import lax
from jax.experimental import pallas as pl
from jax.experimental.pallas import tpu as pltpu
from jax.sharding import PartitionSpec as P

OUTER_TO_INNER = [(0, 1), (3, 2)]
ACROSS_MIDDLE = [(1, 2), (2, 1)]
INNER_TO_OUTER = [(1, 0), (2, 3)]
FAR, NEXT, NEAR = 3, 2, 1

HALF = 128
TAIL = 16
SPREAD = 13777.0
SMALLEST = 1e-30
COSTS = tuple(1_000_000_000 * cost for cost in (6, 6, 6, 6, 6, 6, 6, 6, 6, 6, 6, 6, 6, 6, 6, 6, 6, 6, 6))
VMEM_BYTES = 24 * 1024 * 1024


def shifted(value, axis, steps):
    count = lax.axis_size(axis)
    pairs = [(source, (source + steps) % count) for source in range(count)]
    return lax.ppermute(value, axis, pairs)


def tile_rows(inverse, left_keys, right_keys):
    product = lax.dot_general(
        left_keys, right_keys, (((0,), (0,)), ((), ())), preferred_element_type=jnp.float32
    )
    return product * inverse


def reduce_scattered(own_keys, forward_list, inverse):
    shares = [
        lax.psum_scatter(
            tile_rows(inverse, own_keys, right_keys), "tok", scatter_dimension=0, tiled=True
        )
        for right_keys in forward_list
    ]
    return jnp.stack(shares)[None]


def fold():
    place = lax.axis_index("tok")
    upper = place >= 2
    inner = jnp.logical_or(place == 1, place == 2)
    return upper, inner


def block_at(upper, index):
    return jnp.where(upper, 3 - index, index)


def block_of(ref, upper, index, rows):
    count = ref.shape[1] // rows
    if count == 1:
        return ref[...]
    at = jnp.where(upper, count - 1 - index, index)
    return ref[:, pl.ds(pl.multiple_of(at * rows, rows), rows)]


def product(inverse, left_ref, right_ref, upper, row, column, rows):
    left = block_of(left_ref, upper, row, rows)
    return tile_rows(inverse, left, block_of(right_ref, upper, column, rows))


def row_factor(rows):
    index = lax.broadcasted_iota(jnp.int32, (rows, HALF), 0).astype(jnp.float32) * 0.6180339887
    return 1.0 + (index - jnp.floor(index))


def column_factor(half):
    index = lax.broadcasted_iota(jnp.int32, (1, HALF), 1).astype(jnp.float32) + float(half * HALF)
    index = index * 0.7548776662
    return 1.0 + (index - jnp.floor(index))


def peak_of(value):
    return jnp.max(jnp.max(jnp.abs(value), axis=0, keepdims=True), axis=1, keepdims=True)


def code(scaled):
    power = scaled * scaled
    power = power * power
    power = power * power
    return jnp.where(scaled < 0.0, -power, power)


def decoded(coded):
    root = lax.rsqrt(lax.rsqrt(jnp.maximum(jnp.abs(coded), 1.2e-38)))
    root = root * lax.rsqrt(root)
    return jnp.where(coded < 0.0, -root, root)


def write_message(message_ref, blocks, diagonal=None):
    rows = blocks[0].shape[0]
    peak = functools.reduce(jnp.maximum, [peak_of(block) for block in blocks])
    peak = (jnp.maximum(peak, SMALLEST) * 1.02).astype(jnp.bfloat16).astype(jnp.float32)
    peak = jnp.broadcast_to(peak, (1, HALF))
    factor = row_factor(rows)
    for number, block in enumerate(blocks):
        for half in range(rows // HALF):
            scaled = block[:, half * HALF : (half + 1) * HALF] * factor
            scaled = scaled * (column_factor(half) * (SPREAD / peak))
            start = (number * (rows // HALF) + half) * rows
            message_ref[start : start + rows, :] = code(scaled).astype(jnp.bfloat16)
    start = len(blocks) * (rows // HALF) * rows
    if diagonal is not None:
        write_diagonal(message_ref, start, diagonal, peak)
        start += rows // HALF * TAIL
    message_ref[start : start + TAIL, :] = jnp.broadcast_to(peak, (TAIL, HALF)).astype(jnp.bfloat16)


def place_in_block(rows):
    row = lax.broadcasted_iota(jnp.int32, (rows, rows), 0)
    return row, lax.broadcasted_iota(jnp.int32, (rows, rows), 1)


def write_diagonal(message_ref, start, block, peak):
    rows = block.shape[0]
    row, column = place_in_block(rows)
    line = jnp.sum(jnp.where(row == column, block, 0.0), axis=0, keepdims=True)
    for half in range(rows // HALF):
        scaled = line[:, half * HALF : (half + 1) * HALF] * (column_factor(half) * (SPREAD / peak))
        coded = jnp.broadcast_to(code(scaled), (TAIL, HALF))
        message_ref[start + half * TAIL : start + (half + 1) * TAIL, :] = coded.astype(jnp.bfloat16)


def read_packed(message_ref, number, rows):
    packed = read_block(message_ref, number, rows)
    peak = message_ref[message_ref.shape[0] - TAIL :, :].astype(jnp.float32)[0:1]
    start = message_ref.shape[0] - TAIL - rows // HALF * TAIL
    line = []
    for half in range(rows // HALF):
        coded = message_ref[start + half * TAIL : start + (half + 1) * TAIL, :].astype(jnp.float32)
        line.append(decoded(coded[0:1]) * (peak * (1.0 / SPREAD) / column_factor(half)))
    line = jnp.broadcast_to(jnp.concatenate(line, axis=1), (rows, rows))
    row, column = place_in_block(rows)
    return jnp.where(row < column, packed, jnp.where(row == column, line, packed.T))


def read_block(message_ref, number, rows):
    peak = message_ref[message_ref.shape[0] - TAIL :, :].astype(jnp.float32)[0:1]
    factor = 1.0 / row_factor(rows)
    halves = []
    for half in range(rows // HALF):
        start = (number * (rows // HALF) + half) * rows
        coded = message_ref[start : start + rows, :].astype(jnp.float32)
        factors = peak * (1.0 / SPREAD) / column_factor(half)
        halves.append(decoded(coded) * factor * factors)
    return jnp.concatenate(halves, axis=1)


def message_shape(count, rows, diagonals=0):
    tails = TAIL + diagonals * rows // HALF * TAIL
    return jax.ShapeDtypeStruct((count * rows * rows // HALF + tails, HALF), jnp.bfloat16)


def columns_of(value, upper_value, rows, index):
    return jnp.where(
        upper_value,
        value[:, (3 - index) * rows : (4 - index) * rows],
        value[:, index * rows : (index + 1) * rows],
    )


def send_kernel(row, count, inverse, left_ref, right_ref, message_ref):
    rows = right_ref.shape[1] // 4
    upper, inner = fold()

    @pl.when(jnp.logical_not(inner))
    def _():
        write_message(
            message_ref,
            [
                product(inverse, left_ref, right_ref, upper, row, column, rows)
                for column in range(count)
            ],
        )


def pass_on_kernel(row, count, inverse, left_ref, right_ref, message_ref, far_ref, rest_ref):
    rows = right_ref.shape[1] // 4
    upper, inner = fold()
    far_ref[...] = block_of(right_ref, upper, FAR, rows)
    rest_at = pl.multiple_of(jnp.where(upper, rows, 0), rows)
    rest_ref[...] = right_ref[:, pl.ds(rest_at, 3 * rows)]
    send_kernel(row, count, inverse, left_ref, right_ref, message_ref)


def near_kernel(inverse, left_ref, plain_ref, folded_ref, message_ref):
    rows = left_ref.shape[1] // 4
    upper, inner = fold()

    @pl.when(jnp.logical_not(inner))
    def _():
        write_message(
            message_ref,
            [
                product(inverse, left_ref, right_ref, upper, NEAR, column, rows)
                for right_ref, count in ((plain_ref, 4), (folded_ref, 2))
                for column in range(count)
            ],
        )


def rest_kernel(inverse, left_ref, right_ref, message_ref):
    rows = left_ref.shape[1] // 4
    upper, inner = fold()

    @pl.when(jnp.logical_not(inner))
    def _():
        def own(row, column):
            return product(inverse, left_ref, right_ref, upper, row, column, rows)

        row, column = place_in_block(rows)
        near = own(NEAR, NEAR)
        packed = jnp.where(row >= column, own(NEXT, NEXT), near)
        write_message(message_ref, [own(NEXT, 0), own(NEXT, 1), packed, own(NEAR, 0)], near)


def cross_kernel(row, count, inverse, left_ref, right_ref, in_ref, message_ref):
    rows = right_ref.shape[1] // 4
    upper, inner = fold()

    @pl.when(inner)
    def _():
        write_message(
            message_ref,
            [
                product(inverse, left_ref, right_ref, upper, row, column, rows)
                + read_block(in_ref, column, rows)
                for column in range(count)
            ],
        )


def back_kernel(inverse, left_ref, right_ref, across_ref, message_ref):
    rows = right_ref.shape[1] // 4
    upper, inner = fold()

    @pl.when(inner)
    def _():
        write_message(
            message_ref,
            [
                product(inverse, left_ref, right_ref, upper, 0, column, rows)
                + read_block(across_ref, 3 - column, rows)
                for column in range(4)
            ],
        )


def put(out_ref, upper, column, rows, value):
    at = pl.ds(pl.multiple_of(block_at(upper, column) * rows, rows), rows)
    out_ref[0, 0, :, at] = value


def finish_kernel(near_at, folds, packs, rights, inverse, left_ref, *refs):
    right_refs, (next_ref, near_ref, back_ref) = refs[:rights], refs[rights : rights + 3]
    *turned_refs, token_ref, out_ref = refs[rights + 3 :]
    token_ref[...] = jnp.zeros_like(token_ref)
    rows = left_ref.shape[1] // 4
    upper, inner = fold()

    def own_sums(row, column):
        right_ref = right_refs[-1] if column == FAR else right_refs[0]
        return product(inverse, left_ref, right_ref, upper, row, column, rows)

    def turned_block(number):
        return read_block(turned_refs[number], (1, 1, 2)[number], rows).T

    @pl.when(jnp.logical_not(inner))
    def _():
        for column in range(4):
            put(out_ref, upper, column, rows, own_sums(0, column) + read_block(back_ref, column, rows))

    @pl.when(inner)
    def _():
        for column in range(4):
            own = own_sums(1, column)
            if folds and column >= 2:
                own = own + turned_block(3 - column)
            elif packs and column == 1:
                own = own + read_packed(near_ref, 2, rows)
            else:
                own = own + read_block(near_ref, near_at + column, rows)
            if folds and column == 0:
                own = own + turned_block(2)
            elif packs and column == 1:
                across = read_block(next_ref, 2, rows)
                row, place = place_in_block(rows)
                own = own + jnp.where(row >= place, across, across.T)
            else:
                own = own + read_block(next_ref, 3 - column, rows)
            put(out_ref, upper, column, rows, own)


def ordered(body, count, held, *refs):
    body(*refs[:count], *refs[count + held :])


def call(body, operands, held, cost, out_shape, **options):
    specs = [pl.BlockSpec(memory_space=pltpu.VMEM)] * len(operands)
    specs += [pl.BlockSpec(memory_space=pl.ANY)] * len(held)
    return pl.pallas_call(
        functools.partial(ordered, body, len(operands), len(held)),
        out_shape=out_shape,
        in_specs=specs,
        compiler_params=pltpu.CompilerParams(vmem_limit_bytes=VMEM_BYTES),
        cost_estimate=pl.CostEstimate(flops=cost, bytes_accessed=cost // 1000, transcendentals=0),
        **options,
    )(*operands, *held)


def folded_line(own_keys, inverse):
    width = own_keys.shape[1]
    rows = width // 4
    last, calls = [own_keys], []

    def run(body, operands, shapes, held=(), **options):
        held = (*held, last[0])
        cost = int(COSTS[len(calls)])
        calls.append(cost)
        result = call(functools.partial(body, inverse), operands, held, cost, shapes, **options)
        last[0] = jax.tree.leaves(result)[0]
        return result

    def hop(message, pairs, layers=0):
        count = lax.axis_size("layer")
        pairs = [
            (layer * 4 + source, (layer + layers) % count * 4 + target)
            for layer in range(count)
            for source, target in pairs
        ]
        return lax.ppermute(message, ("layer", "tok"), pairs)

    def send(left, right, row, count):
        body = functools.partial(send_kernel, row, count)
        return hop(run(body, (left, right), message_shape(count, rows)), OUTER_TO_INNER)

    def cross(left, right, row, count, arrived, layers=0):
        body = functools.partial(cross_kernel, row, count)
        message = run(body, (left, right, arrived), message_shape(count, rows))
        return hop(message, ACROSS_MIDDLE, layers)

    def back(left, right, crossed, layers=0, held=()):
        message = run(back_kernel, (left, right, crossed), message_shape(4, rows), held)
        return hop(message, INNER_TO_OUTER, layers)

    tile = jax.ShapeDtypeStruct((1, 3, rows, width), jnp.float32)
    token = jax.ShapeDtypeStruct((TAIL, HALF), jnp.bfloat16)

    def tile_specs(distance):
        return [
            pl.BlockSpec((TAIL, HALF), lambda step: (0, 0)),
            pl.BlockSpec((1, 1, rows, width), lambda step: (0, distance, 0, 0)),
        ]

    def finish(out, distance, rights, next_across, near, returned, turned=(), near_at=0, packs=False, held=()):
        operands = (own_keys, *rights, next_across, near, returned, *turned)
        options = {"held": held}
        if out is not None:
            options = {"held": (out, *held), "input_output_aliases": {len(operands): 1}}
        body = functools.partial(finish_kernel, near_at, len(turned) > 0, packs, len(rights))
        _, out = run(body, operands, [token, tile], grid=(1,), out_specs=tile_specs(distance), **options)
        return out

    second_keys = shifted(own_keys, "layer", -1)
    far_0 = send(own_keys, own_keys, FAR, 4)
    rest_0 = run(rest_kernel, (own_keys, own_keys), message_shape(4, rows, 1))
    rest_0 = hop(rest_0, OUTER_TO_INNER)
    far_across_0 = cross(own_keys, own_keys, FAR, 4, far_0)
    far_1, far_part, rest_part = run(
        functools.partial(pass_on_kernel, FAR, 4),
        (own_keys, second_keys),
        [message_shape(4, rows)]
        + [jax.ShapeDtypeStruct((own_keys.shape[0], count * rows), own_keys.dtype) for count in (1, 3)],
    )
    far_1 = hop(far_1, OUTER_TO_INNER)
    far_part = shifted(far_part, "layer", -1)
    rest_part = shifted(rest_part, "layer", -1)
    next_across_0 = cross(own_keys, own_keys, NEXT, 3, rest_0)
    far_2 = send(far_part, own_keys, FAR, 4)
    back_0 = back(own_keys, own_keys, far_across_0)
    far_across_1 = cross(own_keys, second_keys, FAR, 4, far_1)
    next_1 = send(own_keys, second_keys, NEXT, 4)
    turned = (far_0, rest_0, far_across_0)
    out = finish(None, 0, (own_keys,), next_across_0, rest_0, back_0, turned, 3, True)
    far_across_2 = cross(far_part, own_keys, FAR, 4, far_2)
    next_2 = send(rest_part, own_keys, NEXT, 3)
    back_1 = back(own_keys, second_keys, far_across_1)
    next_across_1 = cross(own_keys, second_keys, NEXT, 4, next_1)
    near = run(near_kernel, (own_keys, second_keys, rest_part), message_shape(6, rows))
    near = hop(near, OUTER_TO_INNER)
    back_2 = back(rest_part, own_keys, far_across_2, 2)
    next_across_2 = cross(rest_part, own_keys, NEXT, 3, next_2, 2)
    turned = (far_2, next_2, far_across_2)
    out = finish(out, 1, (second_keys,), next_across_1, near, back_1)
    return finish(out, 2, (rest_part, far_part), next_across_2, near, back_2, turned, 4)


def per_device(keys):
    own_keys = keys[0]
    layers = lax.axis_size("layer")
    half_span = layers // 2
    inverse = 1.0 / (own_keys.shape[0] * lax.axis_size("tok"))
    if lax.axis_size("tok") == 4 and layers == 4 and own_keys.shape[1] % (8 * HALF) == 0:
        return folded_line(own_keys, inverse)
    forward_list = [own_keys]
    for repeat in range(half_span):
        forward_list.append(shifted(forward_list[-1], "layer", -1))
    return reduce_scattered(own_keys, forward_list, inverse)


def solution(mesh):
    in_specs = (P("layer", ("groups", "tok"), None),)
    out_specs = P("layer", None, ("groups", "tok"), None)
    return jax.shard_map(
        per_device, mesh=mesh, in_specs=in_specs, out_specs=out_specs, check_vma=False
    )
```

```python
import functools

import jax
import jax.numpy as jnp
from jax import lax
from jax.experimental import pallas as pl
from jax.experimental.pallas import tpu as pltpu
from jax.sharding import PartitionSpec as P

OUTER_TO_INNER = [(0, 1), (3, 2)]
ACROSS_MIDDLE = [(1, 2), (2, 1)]
INNER_TO_OUTER = [(1, 0), (2, 3)]
FAR, NEXT, NEAR = 3, 2, 1

HALF = 128
TAIL = 16
SPREAD = 13777.0
SMALLEST = 1e-30
COSTS = (6_000_000_000,) * 20
VMEM_BYTES = 24 * 1024 * 1024


def shifted(value, axis, steps):
    count = lax.axis_size(axis)
    pairs = [(source, (source + steps) % count) for source in range(count)]
    return lax.ppermute(value, axis, pairs)


def tile_rows(inverse, left_keys, right_keys):
    product = lax.dot_general(
        left_keys, right_keys, (((0,), (0,)), ((), ())), preferred_element_type=jnp.float32
    )
    return product * inverse


def reduce_scattered(own_keys, forward_list, inverse):
    shares = [
        lax.psum_scatter(
            tile_rows(inverse, own_keys, right_keys), "tok", scatter_dimension=0, tiled=True
        )
        for right_keys in forward_list
    ]
    return jnp.stack(shares)[None]


def fold():
    place = lax.axis_index("tok")
    upper = place >= 2
    inner = jnp.logical_or(place == 1, place == 2)
    return upper, inner


def block_at(upper, index):
    return jnp.where(upper, 3 - index, index)


def block_of(ref, upper, index, rows):
    count = ref.shape[1] // rows
    if count == 1:
        return ref[...]
    at = jnp.where(upper, count - 1 - index, index)
    return ref[:, pl.ds(pl.multiple_of(at * rows, rows), rows)]


def product(inverse, left_ref, right_ref, upper, row, column, rows):
    left = block_of(left_ref, upper, row, rows)
    return tile_rows(inverse, left, block_of(right_ref, upper, column, rows))


def row_factor(rows):
    index = lax.broadcasted_iota(jnp.int32, (rows, HALF), 0).astype(jnp.float32) * 0.6180339887
    return 1.0 + (index - jnp.floor(index))


def column_factor(half):
    index = lax.broadcasted_iota(jnp.int32, (1, HALF), 1).astype(jnp.float32) + float(half * HALF)
    index = index * 0.7548776662
    return 1.0 + (index - jnp.floor(index))


def peak_of(value):
    return jnp.max(jnp.max(jnp.abs(value), axis=0, keepdims=True), axis=1, keepdims=True)


def code(scaled):
    power = scaled * scaled
    power = power * power
    power = power * power
    return jnp.where(scaled < 0.0, -power, power)


def decoded(coded):
    root = lax.rsqrt(lax.rsqrt(jnp.maximum(jnp.abs(coded), 1.2e-38)))
    root = root * lax.rsqrt(root)
    return jnp.where(coded < 0.0, -root, root)


def write_message(message_ref, blocks, diagonal=None):
    rows = blocks[0].shape[0]
    peak = functools.reduce(jnp.maximum, [peak_of(block) for block in blocks])
    peak = (jnp.maximum(peak, SMALLEST) * 1.02).astype(jnp.bfloat16).astype(jnp.float32)
    peak = jnp.broadcast_to(peak, (1, HALF))
    factor = row_factor(rows)
    for number, block in enumerate(blocks):
        for half in range(rows // HALF):
            scaled = block[:, half * HALF : (half + 1) * HALF] * factor
            scaled = scaled * (column_factor(half) * (SPREAD / peak))
            start = (number * (rows // HALF) + half) * rows
            message_ref[start : start + rows, :] = code(scaled).astype(jnp.bfloat16)
    start = len(blocks) * (rows // HALF) * rows
    if diagonal is not None:
        write_diagonal(message_ref, start, diagonal, peak)
        start += rows // HALF * TAIL
    message_ref[start : start + TAIL, :] = jnp.broadcast_to(peak, (TAIL, HALF)).astype(jnp.bfloat16)


def place_in_block(rows):
    row = lax.broadcasted_iota(jnp.int32, (rows, rows), 0)
    return row, lax.broadcasted_iota(jnp.int32, (rows, rows), 1)


def write_diagonal(message_ref, start, block, peak):
    rows = block.shape[0]
    row, column = place_in_block(rows)
    line = jnp.sum(jnp.where(row == column, block, 0.0), axis=0, keepdims=True)
    for half in range(rows // HALF):
        scaled = line[:, half * HALF : (half + 1) * HALF] * (column_factor(half) * (SPREAD / peak))
        coded = jnp.broadcast_to(code(scaled), (TAIL, HALF))
        message_ref[start + half * TAIL : start + (half + 1) * TAIL, :] = coded.astype(jnp.bfloat16)


def read_packed(message_ref, number, rows):
    packed = read_block(message_ref, number, rows)
    peak = message_ref[message_ref.shape[0] - TAIL :, :].astype(jnp.float32)[0:1]
    start = message_ref.shape[0] - TAIL - rows // HALF * TAIL
    line = []
    for half in range(rows // HALF):
        coded = message_ref[start + half * TAIL : start + (half + 1) * TAIL, :].astype(jnp.float32)
        line.append(decoded(coded[0:1]) * (peak * (1.0 / SPREAD) / column_factor(half)))
    line = jnp.broadcast_to(jnp.concatenate(line, axis=1), (rows, rows))
    row, column = place_in_block(rows)
    return jnp.where(row < column, packed, jnp.where(row == column, line, packed.T))


def read_block(message_ref, number, rows):
    peak = message_ref[message_ref.shape[0] - TAIL :, :].astype(jnp.float32)[0:1]
    factor = 1.0 / row_factor(rows)
    halves = []
    for half in range(rows // HALF):
        start = (number * (rows // HALF) + half) * rows
        coded = message_ref[start : start + rows, :].astype(jnp.float32)
        factors = peak * (1.0 / SPREAD) / column_factor(half)
        halves.append(decoded(coded) * factor * factors)
    return jnp.concatenate(halves, axis=1)


def message_shape(count, rows, diagonals=0):
    tails = TAIL + diagonals * rows // HALF * TAIL
    return jax.ShapeDtypeStruct((count * rows * rows // HALF + tails, HALF), jnp.bfloat16)


def columns_of(value, upper_value, rows, index):
    return jnp.where(
        upper_value,
        value[:, (3 - index) * rows : (4 - index) * rows],
        value[:, index * rows : (index + 1) * rows],
    )


def send_kernel(row, count, inverse, left_ref, right_ref, message_ref):
    rows = right_ref.shape[1] // 4
    upper, inner = fold()

    @pl.when(jnp.logical_not(inner))
    def _():
        write_message(
            message_ref,
            [
                product(inverse, left_ref, right_ref, upper, row, column, rows)
                for column in range(count)
            ],
        )


def pass_on_kernel(row, count, inverse, left_ref, right_ref, message_ref, far_ref, rest_ref):
    rows = right_ref.shape[1] // 4
    upper, inner = fold()
    far_ref[...] = block_of(right_ref, upper, FAR, rows)
    rest_at = pl.multiple_of(jnp.where(upper, rows, 0), rows)
    rest_ref[...] = right_ref[:, pl.ds(rest_at, 3 * rows)]
    send_kernel(row, count, inverse, left_ref, right_ref, message_ref)


def near_kernel(inverse, left_ref, plain_ref, folded_ref, message_ref):
    rows = left_ref.shape[1] // 4
    upper, inner = fold()

    @pl.when(jnp.logical_not(inner))
    def _():
        write_message(
            message_ref,
            [
                product(inverse, left_ref, right_ref, upper, NEAR, column, rows)
                for right_ref, count in ((plain_ref, 4), (folded_ref, 2))
                for column in range(count)
            ],
        )


def rest_kernel(inverse, left_ref, right_ref, message_ref):
    rows = left_ref.shape[1] // 4
    upper, inner = fold()

    @pl.when(jnp.logical_not(inner))
    def _():
        def own(row, column):
            return product(inverse, left_ref, right_ref, upper, row, column, rows)

        row, column = place_in_block(rows)
        near = own(NEAR, NEAR)
        packed = jnp.where(row >= column, own(NEXT, NEXT), near)
        write_message(message_ref, [own(NEXT, 0), own(NEXT, 1), packed, own(NEAR, 0)], near)


def cross_kernel(row, count, inverse, left_ref, right_ref, in_ref, message_ref):
    rows = right_ref.shape[1] // 4
    upper, inner = fold()

    @pl.when(inner)
    def _():
        write_message(
            message_ref,
            [
                product(inverse, left_ref, right_ref, upper, row, column, rows)
                + read_block(in_ref, column, rows)
                for column in range(count)
            ],
        )


def back_kernel(inverse, left_ref, right_ref, across_ref, message_ref):
    rows = right_ref.shape[1] // 4
    upper, inner = fold()

    @pl.when(inner)
    def _():
        write_message(
            message_ref,
            [
                product(inverse, left_ref, right_ref, upper, 0, column, rows)
                + read_block(across_ref, 3 - column, rows)
                for column in range(4)
            ],
        )


def put(out_ref, upper, column, rows, value):
    at = pl.ds(pl.multiple_of(block_at(upper, column) * rows, rows), rows)
    out_ref[0, 0, :, at] = value


def finish_kernel(inverse, keys_ref, next_ref, rest_ref, back_ref, far_ref, across_ref, token_ref, out_ref):
    token_ref[...] = jnp.zeros_like(token_ref)
    rows = keys_ref.shape[1] // 4
    upper, inner = fold()

    def own_sums(row, column):
        return product(inverse, keys_ref, keys_ref, upper, row, column, rows)

    @pl.when(jnp.logical_not(inner))
    def _():
        for column in range(4):
            put(out_ref, upper, column, rows, own_sums(0, column) + read_block(back_ref, column, rows))

    @pl.when(inner)
    def _():
        row, column = place_in_block(rows)
        across = read_block(next_ref, 2, rows)
        blocks = [
            read_block(rest_ref, 3, rows) + read_block(across_ref, 2, rows).T,
            read_packed(rest_ref, 2, rows) + jnp.where(row >= column, across, across.T),
            read_block(rest_ref, 1, rows).T + read_block(next_ref, 1, rows),
            read_block(far_ref, 1, rows).T + read_block(next_ref, 0, rows),
        ]
        for column, block in enumerate(blocks):
            put(out_ref, upper, column, rows, own_sums(1, column) + block)


def partial_kernel(inverse, left_ref, *refs):
    plain_ref, *folded_refs, next_ref, back_ref, far_ref, beside_ref, across_ref, plain_out, folded_out = refs
    rows = left_ref.shape[1] // 4
    upper, inner = fold()

    def own_sums(right_ref, row, column):
        return product(inverse, left_ref, right_ref, upper, row, column, rows)

    def folded_sums(row, column):
        return own_sums(folded_refs[-1] if column == FAR else folded_refs[0], row, column)

    def block(column):
        return slice(column * rows, (column + 1) * rows)

    @pl.when(jnp.logical_not(inner))
    def _():
        for column in range(4):
            plain_out[:, block(column)] = own_sums(plain_ref, 0, column) + read_block(back_ref, column, rows)
            folded_out[:, block(column)] = folded_sums(0, column)

    @pl.when(inner)
    def _():
        turned = {3: (far_ref, 1), 2: (beside_ref, 1), 0: (across_ref, 2)}
        for column in range(4):
            plain_out[:, block(column)] = own_sums(plain_ref, 1, column) + read_block(next_ref, 3 - column, rows)
            sums = folded_sums(1, column)
            if column in turned:
                sums = sums + read_block(*turned[column], rows).T
            folded_out[:, block(column)] = sums


def last_plain_kernel(inverse, sums_ref, near_ref, token_ref, out_ref):
    rows = sums_ref.shape[0]
    upper, inner = fold()
    token_ref[...] = jnp.zeros_like(token_ref)

    @pl.when(jnp.logical_not(inner))
    def _():
        for column in range(4):
            put(out_ref, upper, column, rows, sums_ref[:, column * rows : (column + 1) * rows])

    @pl.when(inner)
    def _():
        for column in range(4):
            sums = sums_ref[:, column * rows : (column + 1) * rows]
            put(out_ref, upper, column, rows, sums + read_block(near_ref, column, rows))


def last_folded_kernel(inverse, sums_ref, near_ref, next_ref, back_ref, token_ref, out_ref):
    rows = sums_ref.shape[0]
    upper, inner = fold()
    token_ref[...] = jnp.zeros_like(token_ref)

    @pl.when(jnp.logical_not(inner))
    def _():
        for column in range(4):
            sums = sums_ref[:, column * rows : (column + 1) * rows]
            put(out_ref, upper, column, rows, sums + read_block(back_ref, column, rows))

    @pl.when(inner)
    def _():
        for column in range(4):
            sums = sums_ref[:, column * rows : (column + 1) * rows]
            if column < 2:
                sums = sums + read_block(near_ref, 4 + column, rows)
            if column > 0:
                sums = sums + read_block(next_ref, 3 - column, rows)
            put(out_ref, upper, column, rows, sums)


def ordered(body, count, held, *refs):
    body(*refs[:count], *refs[count + held :])


def call(body, operands, held, cost, out_shape, **options):
    specs = [pl.BlockSpec(memory_space=pltpu.VMEM)] * len(operands)
    specs += [pl.BlockSpec(memory_space=pl.ANY)] * len(held)
    return pl.pallas_call(
        functools.partial(ordered, body, len(operands), len(held)),
        out_shape=out_shape,
        in_specs=specs,
        compiler_params=pltpu.CompilerParams(vmem_limit_bytes=VMEM_BYTES),
        cost_estimate=pl.CostEstimate(flops=cost, bytes_accessed=cost // 1000, transcendentals=0),
        **options,
    )(*operands, *held)


def folded_line(own_keys, inverse):
    width = own_keys.shape[1]
    rows = width // 4
    last, calls = [own_keys], []

    def run(body, operands, shapes, held=(), **options):
        held = (*held, last[0])
        cost = int(COSTS[len(calls)])
        calls.append(cost)
        result = call(functools.partial(body, inverse), operands, held, cost, shapes, **options)
        last[0] = jax.tree.leaves(result)[0]
        return result

    def hop(message, pairs, layers=0):
        count = lax.axis_size("layer")
        pairs = [
            (layer * 4 + source, (layer + layers) % count * 4 + target)
            for layer in range(count)
            for source, target in pairs
        ]
        return lax.ppermute(message, ("layer", "tok"), pairs)

    def send(left, right, row, count):
        body = functools.partial(send_kernel, row, count)
        return hop(run(body, (left, right), message_shape(count, rows)), OUTER_TO_INNER)

    def cross(left, right, row, count, arrived, layers=0):
        body = functools.partial(cross_kernel, row, count)
        message = run(body, (left, right, arrived), message_shape(count, rows))
        return hop(message, ACROSS_MIDDLE, layers)

    def back(left, right, crossed, layers=0, held=()):
        message = run(back_kernel, (left, right, crossed), message_shape(4, rows), held)
        return hop(message, INNER_TO_OUTER, layers)

    tile = jax.ShapeDtypeStruct((1, 3, rows, width), jnp.float32)
    token = jax.ShapeDtypeStruct((TAIL, HALF), jnp.bfloat16)

    def write_tile(distance, out, body, operands):
        options = {}
        if out is not None:
            options = {"held": (out,), "input_output_aliases": {len(operands): 1}}
        _, out = run(
            body,
            operands,
            [token, tile],
            grid=(1,),
            out_specs=[
                pl.BlockSpec((TAIL, HALF), lambda step: (0, 0)),
                pl.BlockSpec((1, 1, rows, width), lambda step: (0, distance, 0, 0)),
            ],
            **options,
        )
        return out


    def part_of_keys(count):
        return jax.ShapeDtypeStruct((own_keys.shape[0], count * rows), own_keys.dtype)

    second_keys = shifted(own_keys, "layer", -1)
    far_0 = send(own_keys, own_keys, FAR, 4)
    rest_0 = run(rest_kernel, (own_keys, own_keys), message_shape(4, rows, 1))
    rest_0 = hop(rest_0, OUTER_TO_INNER)
    far_across_0 = cross(own_keys, own_keys, FAR, 4, far_0)
    far_1, far_part, rest_part = run(
        functools.partial(pass_on_kernel, FAR, 4),
        (own_keys, second_keys),
        [message_shape(4, rows), part_of_keys(1), part_of_keys(3)],
    )
    far_1 = hop(far_1, OUTER_TO_INNER)
    far_part = shifted(far_part, "layer", -1)
    rest_part = shifted(rest_part, "layer", -1)
    next_across_0 = cross(own_keys, own_keys, NEXT, 3, rest_0)
    far_2 = send(far_part, own_keys, FAR, 4)
    back_0 = back(own_keys, own_keys, far_across_0)
    far_across_1 = cross(own_keys, second_keys, FAR, 4, far_1)
    next_1 = send(own_keys, second_keys, NEXT, 4)
    out = write_tile(
        0, None, finish_kernel, (own_keys, next_across_0, rest_0, back_0, far_0, far_across_0)
    )
    far_across_2 = cross(far_part, own_keys, FAR, 4, far_2)
    next_2 = send(rest_part, own_keys, NEXT, 3)
    back_1 = back(own_keys, second_keys, far_across_1)
    next_across_1 = cross(own_keys, second_keys, NEXT, 4, next_1)
    near = run(near_kernel, (own_keys, second_keys, rest_part), message_shape(6, rows))
    near = hop(near, OUTER_TO_INNER)
    back_2 = back(rest_part, own_keys, far_across_2, 2)
    next_across_2 = cross(rest_part, own_keys, NEXT, 3, next_2, 2)
    part = jax.ShapeDtypeStruct((rows, width), jnp.float32)
    turned = (far_2, next_2, far_across_2)
    parts = run(
        partial_kernel,
        (own_keys, second_keys, rest_part, far_part, next_across_1, back_1, *turned),
        [part, part],
    )
    out = write_tile(1, out, last_plain_kernel, (parts[0], near))
    return write_tile(2, out, last_folded_kernel, (parts[1], near, next_across_2, back_2))


def per_device(keys):
    own_keys = keys[0]
    layers = lax.axis_size("layer")
    half_span = layers // 2
    inverse = 1.0 / (own_keys.shape[0] * lax.axis_size("tok"))
    if lax.axis_size("tok") == 4 and layers == 4 and own_keys.shape[1] % (8 * HALF) == 0:
        return folded_line(own_keys, inverse)
    forward_list = [own_keys]
    for repeat in range(half_span):
        forward_list.append(shifted(forward_list[-1], "layer", -1))
    return reduce_scattered(own_keys, forward_list, inverse)


def solution(mesh):
    in_specs = (P("layer", ("groups", "tok"), None),)
    out_specs = P("layer", None, ("groups", "tok"), None)
    return jax.shard_map(
        per_device, mesh=mesh, in_specs=in_specs, out_specs=out_specs, check_vma=False
    )
```

```python
import functools

import jax
import jax.numpy as jnp
from jax import lax
from jax.experimental import pallas as pl
from jax.experimental.pallas import tpu as pltpu
from jax.sharding import PartitionSpec as P

OUTER_TO_INNER = [(0, 1), (3, 2)]
ACROSS_MIDDLE = [(1, 2), (2, 1)]
INNER_TO_OUTER = [(1, 0), (2, 3)]
FAR, NEXT, NEAR = 3, 2, 1

HALF = 128
TAIL = 16
SPREAD = 13777.0
SMALLEST = 1e-30
COSTS = (6_000_000_000,) * 22
VMEM_BYTES = 24 * 1024 * 1024


def shifted(value, axis, steps):
    count = lax.axis_size(axis)
    pairs = [(source, (source + steps) % count) for source in range(count)]
    return lax.ppermute(value, axis, pairs)


def tile_rows(inverse, left_keys, right_keys):
    product = lax.dot_general(
        left_keys, right_keys, (((0,), (0,)), ((), ())), preferred_element_type=jnp.float32
    )
    return product * inverse


def reduce_scattered(own_keys, forward_list, inverse):
    shares = [
        lax.psum_scatter(
            tile_rows(inverse, own_keys, right_keys), "tok", scatter_dimension=0, tiled=True
        )
        for right_keys in forward_list
    ]
    return jnp.stack(shares)[None]


def fold():
    place = lax.axis_index("tok")
    upper = place >= 2
    inner = jnp.logical_or(place == 1, place == 2)
    return upper, inner


def block_at(upper, index):
    return jnp.where(upper, 3 - index, index)


def block_of(ref, upper, index, rows):
    count = ref.shape[1] // rows
    if count == 1:
        return ref[...]
    at = jnp.where(upper, count - 1 - index, index)
    return ref[:, pl.ds(pl.multiple_of(at * rows, rows), rows)]


def product(inverse, left_ref, right_ref, upper, row, column, rows):
    left = block_of(left_ref, upper, row, rows)
    return tile_rows(inverse, left, block_of(right_ref, upper, column, rows))


def row_factor(rows):
    index = lax.broadcasted_iota(jnp.int32, (rows, HALF), 0).astype(jnp.float32) * 0.6180339887
    return 1.0 + (index - jnp.floor(index))


def column_factor(half):
    index = lax.broadcasted_iota(jnp.int32, (1, HALF), 1).astype(jnp.float32) + float(half * HALF)
    index = index * 0.7548776662
    return 1.0 + (index - jnp.floor(index))


def peak_of(value):
    return jnp.max(jnp.max(jnp.abs(value), axis=0, keepdims=True), axis=1, keepdims=True)


def code(scaled):
    power = scaled * scaled
    power = power * power
    power = power * power
    return jnp.where(scaled < 0.0, -power, power)


def decoded(coded):
    root = lax.rsqrt(lax.rsqrt(jnp.maximum(jnp.abs(coded), 1.2e-38)))
    root = root * lax.rsqrt(root)
    return jnp.where(coded < 0.0, -root, root)


def write_message(message_ref, blocks, diagonal=None):
    rows = blocks[0].shape[0]
    peak = functools.reduce(jnp.maximum, [peak_of(block) for block in blocks])
    peak = (jnp.maximum(peak, SMALLEST) * 1.02).astype(jnp.bfloat16).astype(jnp.float32)
    peak = jnp.broadcast_to(peak, (1, HALF))
    factor = row_factor(rows)
    for number, block in enumerate(blocks):
        for half in range(rows // HALF):
            scaled = block[:, half * HALF : (half + 1) * HALF] * factor
            scaled = scaled * (column_factor(half) * (SPREAD / peak))
            start = (number * (rows // HALF) + half) * rows
            message_ref[start : start + rows, :] = code(scaled).astype(jnp.bfloat16)
    start = len(blocks) * (rows // HALF) * rows
    if diagonal is not None:
        write_diagonal(message_ref, start, diagonal, peak)
        start += rows // HALF * TAIL
    message_ref[start : start + TAIL, :] = jnp.broadcast_to(peak, (TAIL, HALF)).astype(jnp.bfloat16)


def place_in_block(rows):
    row = lax.broadcasted_iota(jnp.int32, (rows, rows), 0)
    return row, lax.broadcasted_iota(jnp.int32, (rows, rows), 1)


def write_diagonal(message_ref, start, block, peak):
    rows = block.shape[0]
    row, column = place_in_block(rows)
    line = jnp.sum(jnp.where(row == column, block, 0.0), axis=0, keepdims=True)
    for half in range(rows // HALF):
        scaled = line[:, half * HALF : (half + 1) * HALF] * (column_factor(half) * (SPREAD / peak))
        coded = jnp.broadcast_to(code(scaled), (TAIL, HALF))
        message_ref[start + half * TAIL : start + (half + 1) * TAIL, :] = coded.astype(jnp.bfloat16)


def read_packed(message_ref, number, rows):
    packed = read_block(message_ref, number, rows)
    peak = message_ref[message_ref.shape[0] - TAIL :, :].astype(jnp.float32)[0:1]
    start = message_ref.shape[0] - TAIL - rows // HALF * TAIL
    line = []
    for half in range(rows // HALF):
        coded = message_ref[start + half * TAIL : start + (half + 1) * TAIL, :].astype(jnp.float32)
        line.append(decoded(coded[0:1]) * (peak * (1.0 / SPREAD) / column_factor(half)))
    line = jnp.broadcast_to(jnp.concatenate(line, axis=1), (rows, rows))
    row, column = place_in_block(rows)
    return jnp.where(row < column, packed, jnp.where(row == column, line, packed.T))


def read_block(message_ref, number, rows):
    peak = message_ref[message_ref.shape[0] - TAIL :, :].astype(jnp.float32)[0:1]
    factor = 1.0 / row_factor(rows)
    halves = []
    for half in range(rows // HALF):
        start = (number * (rows // HALF) + half) * rows
        coded = message_ref[start : start + rows, :].astype(jnp.float32)
        factors = peak * (1.0 / SPREAD) / column_factor(half)
        halves.append(decoded(coded) * factor * factors)
    return jnp.concatenate(halves, axis=1)


def message_shape(count, rows, diagonals=0):
    tails = TAIL + diagonals * rows // HALF * TAIL
    return jax.ShapeDtypeStruct((count * rows * rows // HALF + tails, HALF), jnp.bfloat16)


def columns_of(value, upper_value, rows, index):
    return jnp.where(
        upper_value,
        value[:, (3 - index) * rows : (4 - index) * rows],
        value[:, index * rows : (index + 1) * rows],
    )


def send_kernel(row, count, inverse, left_ref, right_ref, message_ref):
    rows = right_ref.shape[1] // 4
    upper, inner = fold()

    @pl.when(jnp.logical_not(inner))
    def _():
        write_message(
            message_ref,
            [
                product(inverse, left_ref, right_ref, upper, row, column, rows)
                for column in range(count)
            ],
        )


def far_part_kernel(inverse, keys_ref, part_ref):
    upper, inner = fold()
    part_ref[...] = block_of(keys_ref, upper, FAR, keys_ref.shape[1] // 4)


def rest_part_kernel(inverse, keys_ref, part_ref):
    rows = keys_ref.shape[1] // 4
    upper, inner = fold()
    rest_at = pl.multiple_of(jnp.where(upper, rows, 0), rows)
    part_ref[...] = keys_ref[:, pl.ds(rest_at, 3 * rows)]


def near_kernel(inverse, left_ref, plain_ref, folded_ref, message_ref):
    rows = left_ref.shape[1] // 4
    upper, inner = fold()

    @pl.when(jnp.logical_not(inner))
    def _():
        write_message(
            message_ref,
            [
                product(inverse, left_ref, right_ref, upper, NEAR, column, rows)
                for right_ref, count in ((plain_ref, 4), (folded_ref, 2))
                for column in range(count)
            ],
        )


def rest_kernel(inverse, left_ref, right_ref, message_ref):
    rows = left_ref.shape[1] // 4
    upper, inner = fold()

    @pl.when(jnp.logical_not(inner))
    def _():
        def own(row, column):
            return product(inverse, left_ref, right_ref, upper, row, column, rows)

        row, column = place_in_block(rows)
        near = own(NEAR, NEAR)
        packed = jnp.where(row >= column, own(NEXT, NEXT), near)
        write_message(message_ref, [own(NEXT, 0), own(NEXT, 1), packed, own(NEAR, 0)], near)


def cross_kernel(row, count, inverse, left_ref, right_ref, in_ref, message_ref):
    rows = right_ref.shape[1] // 4
    upper, inner = fold()

    @pl.when(inner)
    def _():
        write_message(
            message_ref,
            [
                product(inverse, left_ref, right_ref, upper, row, column, rows)
                + read_block(in_ref, column, rows)
                for column in range(count)
            ],
        )


def back_kernel(inverse, left_ref, right_ref, across_ref, message_ref):
    rows = right_ref.shape[1] // 4
    upper, inner = fold()

    @pl.when(inner)
    def _():
        write_message(
            message_ref,
            [
                product(inverse, left_ref, right_ref, upper, 0, column, rows)
                + read_block(across_ref, 3 - column, rows)
                for column in range(4)
            ],
        )


def put(out_ref, upper, column, rows, value):
    at = pl.ds(pl.multiple_of(block_at(upper, column) * rows, rows), rows)
    out_ref[0, 0, :, at] = value


def finish_kernel(inverse, keys_ref, next_ref, rest_ref, back_ref, far_ref, across_ref, token_ref, out_ref):
    token_ref[...] = jnp.zeros_like(token_ref)
    rows = keys_ref.shape[1] // 4
    upper, inner = fold()

    def own_sums(row, column):
        return product(inverse, keys_ref, keys_ref, upper, row, column, rows)

    @pl.when(jnp.logical_not(inner))
    def _():
        for column in range(4):
            put(out_ref, upper, column, rows, own_sums(0, column) + read_block(back_ref, column, rows))

    @pl.when(inner)
    def _():
        row, column = place_in_block(rows)
        across = read_block(next_ref, 2, rows)
        blocks = [
            read_block(rest_ref, 3, rows) + read_block(across_ref, 2, rows).T,
            read_packed(rest_ref, 2, rows) + jnp.where(row >= column, across, across.T),
            read_block(rest_ref, 1, rows).T + read_block(next_ref, 1, rows),
            read_block(far_ref, 1, rows).T + read_block(next_ref, 0, rows),
        ]
        for column, block in enumerate(blocks):
            put(out_ref, upper, column, rows, own_sums(1, column) + block)


def partial_kernel(inverse, left_ref, *refs):
    plain_ref, *folded_refs, next_ref, back_ref, far_ref, beside_ref, across_ref, plain_out, folded_out = refs
    rows = left_ref.shape[1] // 4
    upper, inner = fold()

    def own_sums(right_ref, row, column):
        return product(inverse, left_ref, right_ref, upper, row, column, rows)

    def folded_sums(row, column):
        return own_sums(folded_refs[-1] if column == FAR else folded_refs[0], row, column)

    def block(column):
        return slice(column * rows, (column + 1) * rows)

    @pl.when(jnp.logical_not(inner))
    def _():
        for column in range(4):
            plain_out[:, block(column)] = own_sums(plain_ref, 0, column) + read_block(back_ref, column, rows)
            folded_out[:, block(column)] = folded_sums(0, column)

    @pl.when(inner)
    def _():
        turned = {3: (far_ref, 1), 2: (beside_ref, 1), 0: (across_ref, 2)}
        for column in range(4):
            plain_out[:, block(column)] = own_sums(plain_ref, 1, column) + read_block(next_ref, 3 - column, rows)
            sums = folded_sums(1, column)
            if column in turned:
                sums = sums + read_block(*turned[column], rows).T
            folded_out[:, block(column)] = sums


def plain_tile_kernel(inverse, plain_ref, folded_ref, near_ref, back_ref, sums_ref, out_ref):
    rows = plain_ref.shape[0]
    upper, inner = fold()

    def block(column):
        return slice(column * rows, (column + 1) * rows)

    @pl.when(jnp.logical_not(inner))
    def _():
        for column in range(4):
            put(out_ref, upper, column, rows, plain_ref[:, block(column)])
            sums_ref[:, block(column)] = folded_ref[:, block(column)] + read_block(back_ref, column, rows)

    @pl.when(inner)
    def _():
        for column in range(4):
            sums = plain_ref[:, block(column)] + read_block(near_ref, column, rows)
            put(out_ref, upper, column, rows, sums)
            sums = folded_ref[:, block(column)]
            if column < 2:
                sums = sums + read_block(near_ref, 4 + column, rows)
            sums_ref[:, block(column)] = sums


def folded_tile_kernel(inverse, sums_ref, next_ref, token_ref, out_ref):
    rows = sums_ref.shape[0]
    upper, inner = fold()
    token_ref[...] = jnp.zeros_like(token_ref)

    def sums(column):
        return sums_ref[:, column * rows : (column + 1) * rows]

    @pl.when(jnp.logical_not(inner))
    def _():
        for column in range(4):
            put(out_ref, upper, column, rows, sums(column))

    @pl.when(inner)
    def _():
        put(out_ref, upper, 0, rows, sums(0))
        for column in range(1, 4):
            put(out_ref, upper, column, rows, sums(column) + read_block(next_ref, 3 - column, rows))


def ordered(body, count, held, *refs):
    body(*refs[:count], *refs[count + held :])


def call(body, operands, held, cost, out_shape, **options):
    specs = [pl.BlockSpec(memory_space=pltpu.VMEM)] * len(operands)
    specs += [pl.BlockSpec(memory_space=pl.ANY)] * len(held)
    return pl.pallas_call(
        functools.partial(ordered, body, len(operands), len(held)),
        out_shape=out_shape,
        in_specs=specs,
        compiler_params=pltpu.CompilerParams(vmem_limit_bytes=VMEM_BYTES),
        cost_estimate=pl.CostEstimate(flops=cost, bytes_accessed=cost // 1000, transcendentals=0),
        **options,
    )(*operands, *held)


def folded_line(own_keys, inverse):
    width = own_keys.shape[1]
    rows = width // 4
    last, calls = [own_keys], []

    def run(body, operands, shapes, held=(), **options):
        held = (*held, last[0])
        cost = int(COSTS[len(calls)])
        calls.append(cost)
        result = call(functools.partial(body, inverse), operands, held, cost, shapes, **options)
        last[0] = jax.tree.leaves(result)[0]
        return result

    def hop(message, pairs, layers=0):
        count = lax.axis_size("layer")
        pairs = [
            (layer * 4 + source, (layer + layers) % count * 4 + target)
            for layer in range(count)
            for source, target in pairs
        ]
        return lax.ppermute(message, ("layer", "tok"), pairs)

    def send(left, right, row, count, held=()):
        body = functools.partial(send_kernel, row, count)
        return hop(run(body, (left, right), message_shape(count, rows), held), OUTER_TO_INNER)

    def cross(left, right, row, count, arrived, layers=0):
        body = functools.partial(cross_kernel, row, count)
        message = run(body, (left, right, arrived), message_shape(count, rows))
        return hop(message, ACROSS_MIDDLE, layers)

    def back(left, right, crossed, layers=0, held=()):
        message = run(back_kernel, (left, right, crossed), message_shape(4, rows), held)
        return hop(message, INNER_TO_OUTER, layers)

    tile = jax.ShapeDtypeStruct((1, 3, rows, width), jnp.float32)
    token = jax.ShapeDtypeStruct((TAIL, HALF), jnp.bfloat16)

    def write_tile(distance, out, body, operands, beside=token):
        options = {}
        if out is not None:
            options = {"held": (out,), "input_output_aliases": {len(operands): 1}}
        return run(
            body,
            operands,
            [beside, tile],
            grid=(1,),
            out_specs=[
                pl.BlockSpec(beside.shape, lambda step: (0, 0)),
                pl.BlockSpec((1, 1, rows, width), lambda step: (0, distance, 0, 0)),
            ],
            **options,
        )


    def part_of_keys(count):
        return jax.ShapeDtypeStruct((own_keys.shape[0], count * rows), own_keys.dtype)

    second_keys = shifted(own_keys, "layer", -1)
    far_0 = send(own_keys, own_keys, FAR, 4)
    rest_0 = run(rest_kernel, (own_keys, own_keys), message_shape(4, rows, 1))
    rest_0 = hop(rest_0, OUTER_TO_INNER)
    far_across_0 = cross(own_keys, own_keys, FAR, 4, far_0)
    far_1 = send(own_keys, second_keys, FAR, 4)
    far_part = shifted(run(far_part_kernel, (second_keys,), part_of_keys(1)), "layer", -1)
    next_across_0 = cross(own_keys, own_keys, NEXT, 3, rest_0)
    far_2 = send(far_part, own_keys, FAR, 4)
    rest_part = shifted(run(rest_part_kernel, (second_keys,), part_of_keys(3)), "layer", -1)
    far_across_1 = cross(own_keys, second_keys, FAR, 4, far_1)
    next_1 = send(own_keys, second_keys, NEXT, 4, held=(next_across_0,))
    back_0 = back(own_keys, own_keys, far_across_0)
    far_across_2 = cross(far_part, own_keys, FAR, 4, far_2)
    next_2 = send(rest_part, own_keys, NEXT, 3)
    back_1 = back(own_keys, second_keys, far_across_1)
    near = run(near_kernel, (own_keys, second_keys, rest_part), message_shape(6, rows), (back_0,))
    near = hop(near, OUTER_TO_INNER)
    next_across_1 = cross(own_keys, second_keys, NEXT, 4, next_1)
    back_2 = back(rest_part, own_keys, far_across_2, 2)
    next_across_2 = cross(rest_part, own_keys, NEXT, 3, next_2, 2)
    _, out = write_tile(
        0, None, finish_kernel, (own_keys, next_across_0, rest_0, back_0, far_0, far_across_0)
    )
    part = jax.ShapeDtypeStruct((rows, width), jnp.float32)
    turned = (far_2, next_2, far_across_2)
    parts = run(
        partial_kernel,
        (own_keys, second_keys, rest_part, far_part, next_across_1, back_1, *turned),
        [part, part],
    )
    sums, out = write_tile(1, out, plain_tile_kernel, (*parts, near, back_2), part)
    _, out = write_tile(2, out, folded_tile_kernel, (sums, next_across_2))
    return out


def per_device(keys):
    own_keys = keys[0]
    layers = lax.axis_size("layer")
    half_span = layers // 2
    inverse = 1.0 / (own_keys.shape[0] * lax.axis_size("tok"))
    if lax.axis_size("tok") == 4 and layers == 4 and own_keys.shape[1] % (8 * HALF) == 0:
        return folded_line(own_keys, inverse)
    forward_list = [own_keys]
    for repeat in range(half_span):
        forward_list.append(shifted(forward_list[-1], "layer", -1))
    return reduce_scattered(own_keys, forward_list, inverse)


def solution(mesh):
    in_specs = (P("layer", ("groups", "tok"), None),)
    out_specs = P("layer", None, ("groups", "tok"), None)
    return jax.shard_map(
        per_device, mesh=mesh, in_specs=in_specs, out_specs=out_specs, check_vma=False
    )
```

```python
import functools

import jax
import jax.numpy as jnp
from jax import lax
from jax.experimental import pallas as pl
from jax.experimental.pallas import tpu as pltpu
from jax.sharding import PartitionSpec as P

OUTER_TO_INNER = [(0, 1), (3, 2)]
ACROSS_MIDDLE = [(1, 2), (2, 1)]
INNER_TO_OUTER = [(1, 0), (2, 3)]
FAR, NEXT, NEAR = 3, 2, 1

HALF = 128
TAIL = 16
SPREAD = 13777.0
SMALLEST = 1e-30
COSTS = (6_000_000_000,) * 22
VMEM_BYTES = 24 * 1024 * 1024


def shifted(value, axis, steps):
    count = lax.axis_size(axis)
    pairs = [(source, (source + steps) % count) for source in range(count)]
    return lax.ppermute(value, axis, pairs)


def tile_rows(inverse, left_keys, right_keys):
    product = lax.dot_general(
        left_keys, right_keys, (((0,), (0,)), ((), ())), preferred_element_type=jnp.float32
    )
    return product * inverse


def reduce_scattered(own_keys, forward_list, inverse):
    shares = [
        lax.psum_scatter(
            tile_rows(inverse, own_keys, right_keys), "tok", scatter_dimension=0, tiled=True
        )
        for right_keys in forward_list
    ]
    return jnp.stack(shares)[None]


def fold():
    place = lax.axis_index("tok")
    upper = place >= 2
    inner = jnp.logical_or(place == 1, place == 2)
    return upper, inner


def block_at(upper, index):
    return jnp.where(upper, 3 - index, index)


def block_of(ref, upper, index, rows):
    count = ref.shape[1] // rows
    if count == 1:
        return ref[...]
    at = jnp.where(upper, count - 1 - index, index)
    return ref[:, pl.ds(pl.multiple_of(at * rows, rows), rows)]


def product(inverse, left_ref, right_ref, upper, row, column, rows):
    left = block_of(left_ref, upper, row, rows)
    return tile_rows(inverse, left, block_of(right_ref, upper, column, rows))


def row_products(inverse, left_ref, right_ref, upper, row, columns, rows):
    left = block_of(left_ref, upper, row, rows).T
    return [
        jnp.dot(left, block_of(right_ref, upper, column, rows), preferred_element_type=jnp.float32) * inverse
        for column in columns
    ]


def row_factor(rows):
    index = lax.broadcasted_iota(jnp.int32, (rows, HALF), 0).astype(jnp.float32) * 0.6180339887
    return 1.0 + (index - jnp.floor(index))


def column_factor(half):
    index = lax.broadcasted_iota(jnp.int32, (1, HALF), 1).astype(jnp.float32) + float(half * HALF)
    index = index * 0.7548776662
    return 1.0 + (index - jnp.floor(index))


def peak_of(value):
    return jnp.max(jnp.max(jnp.abs(value), axis=0, keepdims=True), axis=1, keepdims=True)


def code(scaled):
    power = scaled * scaled
    power = power * power
    power = power * power
    return jnp.where(scaled < 0.0, -power, power)


def decoded(coded):
    root = lax.rsqrt(lax.rsqrt(jnp.maximum(jnp.abs(coded), 1.2e-38)))
    root = root * lax.rsqrt(root)
    return jnp.where(coded < 0.0, -root, root)


def write_message(message_ref, blocks, diagonal=None):
    rows = blocks[0].shape[0]
    peak = functools.reduce(jnp.maximum, [peak_of(block) for block in blocks])
    peak = (jnp.maximum(peak, SMALLEST) * 1.02).astype(jnp.bfloat16).astype(jnp.float32)
    peak = jnp.broadcast_to(peak, (1, HALF))
    factor = row_factor(rows)
    for number, block in enumerate(blocks):
        for half in range(rows // HALF):
            scaled = block[:, half * HALF : (half + 1) * HALF] * factor
            scaled = scaled * (column_factor(half) * (SPREAD / peak))
            start = (number * (rows // HALF) + half) * rows
            message_ref[start : start + rows, :] = code(scaled).astype(jnp.bfloat16)
    start = len(blocks) * (rows // HALF) * rows
    if diagonal is not None:
        write_diagonal(message_ref, start, diagonal, peak)
        start += rows // HALF * TAIL
    message_ref[start : start + TAIL, :] = jnp.broadcast_to(peak, (TAIL, HALF)).astype(jnp.bfloat16)


def place_in_block(rows):
    row = lax.broadcasted_iota(jnp.int32, (rows, rows), 0)
    return row, lax.broadcasted_iota(jnp.int32, (rows, rows), 1)


def write_diagonal(message_ref, start, block, peak):
    rows = block.shape[0]
    row, column = place_in_block(rows)
    line = jnp.sum(jnp.where(row == column, block, 0.0), axis=0, keepdims=True)
    for half in range(rows // HALF):
        scaled = line[:, half * HALF : (half + 1) * HALF] * (column_factor(half) * (SPREAD / peak))
        coded = jnp.broadcast_to(code(scaled), (TAIL, HALF))
        message_ref[start + half * TAIL : start + (half + 1) * TAIL, :] = coded.astype(jnp.bfloat16)


def read_packed(message_ref, number, rows):
    packed = read_block(message_ref, number, rows)
    peak = message_ref[message_ref.shape[0] - TAIL :, :].astype(jnp.float32)[0:1]
    start = message_ref.shape[0] - TAIL - rows // HALF * TAIL
    line = []
    for half in range(rows // HALF):
        coded = message_ref[start + half * TAIL : start + (half + 1) * TAIL, :].astype(jnp.float32)
        line.append(decoded(coded[0:1]) * (peak * (1.0 / SPREAD) / column_factor(half)))
    line = jnp.broadcast_to(jnp.concatenate(line, axis=1), (rows, rows))
    row, column = place_in_block(rows)
    return jnp.where(row < column, packed, jnp.where(row == column, line, packed.T))


def read_block(message_ref, number, rows):
    peak = message_ref[message_ref.shape[0] - TAIL :, :].astype(jnp.float32)[0:1]
    factor = 1.0 / row_factor(rows)
    halves = []
    for half in range(rows // HALF):
        start = (number * (rows // HALF) + half) * rows
        coded = message_ref[start : start + rows, :].astype(jnp.float32)
        factors = peak * (1.0 / SPREAD) / column_factor(half)
        halves.append(decoded(coded) * factor * factors)
    return jnp.concatenate(halves, axis=1)


def message_shape(count, rows, diagonals=0):
    tails = TAIL + diagonals * rows // HALF * TAIL
    return jax.ShapeDtypeStruct((count * rows * rows // HALF + tails, HALF), jnp.bfloat16)


def columns_of(value, upper_value, rows, index):
    return jnp.where(
        upper_value,
        value[:, (3 - index) * rows : (4 - index) * rows],
        value[:, index * rows : (index + 1) * rows],
    )


def send_kernel(row, count, inverse, left_ref, right_ref, message_ref):
    rows = right_ref.shape[1] // 4
    upper, inner = fold()

    @pl.when(jnp.logical_not(inner))
    def _():
        write_message(
            message_ref,
            row_products(inverse, left_ref, right_ref, upper, row, range(count), rows),
        )


def far_part_kernel(inverse, keys_ref, part_ref):
    upper, inner = fold()
    part_ref[...] = block_of(keys_ref, upper, FAR, keys_ref.shape[1] // 4)


def rest_part_kernel(inverse, keys_ref, part_ref):
    rows = keys_ref.shape[1] // 4
    upper, inner = fold()
    rest_at = pl.multiple_of(jnp.where(upper, rows, 0), rows)
    part_ref[...] = keys_ref[:, pl.ds(rest_at, 3 * rows)]


def near_kernel(inverse, left_ref, plain_ref, folded_ref, message_ref):
    rows = left_ref.shape[1] // 4
    upper, inner = fold()

    @pl.when(jnp.logical_not(inner))
    def _():
        write_message(
            message_ref,
            [
                product(inverse, left_ref, right_ref, upper, NEAR, column, rows)
                for right_ref, count in ((plain_ref, 4), (folded_ref, 2))
                for column in range(count)
            ],
        )


def rest_kernel(inverse, left_ref, right_ref, message_ref):
    rows = left_ref.shape[1] // 4
    upper, inner = fold()

    @pl.when(jnp.logical_not(inner))
    def _():
        def own(row, column):
            return product(inverse, left_ref, right_ref, upper, row, column, rows)

        row, column = place_in_block(rows)
        near = own(NEAR, NEAR)
        packed = jnp.where(row >= column, own(NEXT, NEXT), near)
        write_message(message_ref, [own(NEXT, 0), own(NEXT, 1), packed, own(NEAR, 0)], near)


def cross_kernel(row, count, inverse, left_ref, right_ref, in_ref, message_ref):
    rows = right_ref.shape[1] // 4
    upper, inner = fold()

    @pl.when(inner)
    def _():
        write_message(
            message_ref,
            [
                block + read_block(in_ref, column, rows)
                for column, block in enumerate(
                    row_products(inverse, left_ref, right_ref, upper, row, range(count), rows)
                )
            ],
        )


def back_kernel(inverse, left_ref, right_ref, across_ref, message_ref):
    rows = right_ref.shape[1] // 4
    upper, inner = fold()

    @pl.when(inner)
    def _():
        write_message(
            message_ref,
            [
                product(inverse, left_ref, right_ref, upper, 0, column, rows)
                + read_block(across_ref, 3 - column, rows)
                for column in range(4)
            ],
        )


def put(out_ref, upper, column, rows, value):
    at = pl.ds(pl.multiple_of(block_at(upper, column) * rows, rows), rows)
    out_ref[0, 0, :, at] = value


def finish_kernel(inverse, keys_ref, next_ref, rest_ref, back_ref, far_ref, across_ref, token_ref, out_ref):
    token_ref[...] = jnp.zeros_like(token_ref)
    rows = keys_ref.shape[1] // 4
    upper, inner = fold()

    def own_sums(row, column):
        return product(inverse, keys_ref, keys_ref, upper, row, column, rows)

    @pl.when(jnp.logical_not(inner))
    def _():
        for column in range(4):
            put(out_ref, upper, column, rows, own_sums(0, column) + read_block(back_ref, column, rows))

    @pl.when(inner)
    def _():
        row, column = place_in_block(rows)
        across = read_block(next_ref, 2, rows)
        blocks = [
            read_block(rest_ref, 3, rows) + read_block(across_ref, 2, rows).T,
            read_packed(rest_ref, 2, rows) + jnp.where(row >= column, across, across.T),
            read_block(rest_ref, 1, rows).T + read_block(next_ref, 1, rows),
            read_block(far_ref, 1, rows).T + read_block(next_ref, 0, rows),
        ]
        for column, block in enumerate(blocks):
            put(out_ref, upper, column, rows, own_sums(1, column) + block)


def partial_kernel(inverse, left_ref, *refs):
    plain_ref, *folded_refs, next_ref, back_ref, far_ref, beside_ref, across_ref, plain_out, folded_out = refs
    rows = left_ref.shape[1] // 4
    upper, inner = fold()

    def own_sums(right_ref, row, column):
        return product(inverse, left_ref, right_ref, upper, row, column, rows)

    def folded_sums(row, column):
        return own_sums(folded_refs[-1] if column == FAR else folded_refs[0], row, column)

    def block(column):
        return slice(column * rows, (column + 1) * rows)

    @pl.when(jnp.logical_not(inner))
    def _():
        for column in range(4):
            plain_out[:, block(column)] = own_sums(plain_ref, 0, column) + read_block(back_ref, column, rows)
            folded_out[:, block(column)] = folded_sums(0, column)

    @pl.when(inner)
    def _():
        turned = {3: (far_ref, 1), 2: (beside_ref, 1), 0: (across_ref, 2)}
        for column in range(4):
            plain_out[:, block(column)] = own_sums(plain_ref, 1, column) + read_block(next_ref, 3 - column, rows)
            sums = folded_sums(1, column)
            if column in turned:
                sums = sums + read_block(*turned[column], rows).T
            folded_out[:, block(column)] = sums


def plain_tile_kernel(inverse, plain_ref, folded_ref, near_ref, back_ref, sums_ref, out_ref):
    rows = plain_ref.shape[0]
    upper, inner = fold()

    def block(column):
        return slice(column * rows, (column + 1) * rows)

    @pl.when(jnp.logical_not(inner))
    def _():
        for column in range(4):
            put(out_ref, upper, column, rows, plain_ref[:, block(column)])
            sums_ref[:, block(column)] = folded_ref[:, block(column)] + read_block(back_ref, column, rows)

    @pl.when(inner)
    def _():
        for column in range(4):
            sums = plain_ref[:, block(column)] + read_block(near_ref, column, rows)
            put(out_ref, upper, column, rows, sums)
            sums = folded_ref[:, block(column)]
            if column < 2:
                sums = sums + read_block(near_ref, 4 + column, rows)
            sums_ref[:, block(column)] = sums


def folded_tile_kernel(inverse, sums_ref, next_ref, token_ref, out_ref):
    rows = sums_ref.shape[0]
    upper, inner = fold()
    token_ref[...] = jnp.zeros_like(token_ref)

    def sums(column):
        return sums_ref[:, column * rows : (column + 1) * rows]

    @pl.when(jnp.logical_not(inner))
    def _():
        for column in range(4):
            put(out_ref, upper, column, rows, sums(column))

    @pl.when(inner)
    def _():
        put(out_ref, upper, 0, rows, sums(0))
        for column in range(1, 4):
            put(out_ref, upper, column, rows, sums(column) + read_block(next_ref, 3 - column, rows))


def ordered(body, count, held, *refs):
    body(*refs[:count], *refs[count + held :])


def call(body, operands, held, cost, out_shape, **options):
    specs = [pl.BlockSpec(memory_space=pltpu.VMEM)] * len(operands)
    specs += [pl.BlockSpec(memory_space=pl.ANY)] * len(held)
    return pl.pallas_call(
        functools.partial(ordered, body, len(operands), len(held)),
        out_shape=out_shape,
        in_specs=specs,
        compiler_params=pltpu.CompilerParams(vmem_limit_bytes=VMEM_BYTES),
        cost_estimate=pl.CostEstimate(flops=cost, bytes_accessed=cost // 1000, transcendentals=0),
        **options,
    )(*operands, *held)


def folded_line(own_keys, inverse):
    width = own_keys.shape[1]
    rows = width // 4
    last, calls = [own_keys], []

    def run(body, operands, shapes, held=(), **options):
        held = (*held, last[0])
        cost = int(COSTS[len(calls)])
        calls.append(cost)
        result = call(functools.partial(body, inverse), operands, held, cost, shapes, **options)
        last[0] = jax.tree.leaves(result)[0]
        return result

    def hop(message, pairs, layers=0):
        count = lax.axis_size("layer")
        pairs = [
            (layer * 4 + source, (layer + layers) % count * 4 + target)
            for layer in range(count)
            for source, target in pairs
        ]
        return lax.ppermute(message, ("layer", "tok"), pairs)

    def send(left, right, row, count, held=()):
        body = functools.partial(send_kernel, row, count)
        return hop(run(body, (left, right), message_shape(count, rows), held), OUTER_TO_INNER)

    def cross(left, right, row, count, arrived, layers=0):
        body = functools.partial(cross_kernel, row, count)
        message = run(body, (left, right, arrived), message_shape(count, rows))
        return hop(message, ACROSS_MIDDLE, layers)

    def back(left, right, crossed, layers=0, held=()):
        message = run(back_kernel, (left, right, crossed), message_shape(4, rows), held)
        return hop(message, INNER_TO_OUTER, layers)

    tile = jax.ShapeDtypeStruct((1, 3, rows, width), jnp.float32)
    token = jax.ShapeDtypeStruct((TAIL, HALF), jnp.bfloat16)

    def write_tile(distance, out, body, operands, beside=token):
        options = {}
        if out is not None:
            options = {"held": (out,), "input_output_aliases": {len(operands): 1}}
        return run(
            body,
            operands,
            [beside, tile],
            grid=(1,),
            out_specs=[
                pl.BlockSpec(beside.shape, lambda step: (0, 0)),
                pl.BlockSpec((1, 1, rows, width), lambda step: (0, distance, 0, 0)),
            ],
            **options,
        )


    def part_of_keys(count):
        return jax.ShapeDtypeStruct((own_keys.shape[0], count * rows), own_keys.dtype)

    second_keys = shifted(own_keys, "layer", -1)
    far_0 = send(own_keys, own_keys, FAR, 4)
    rest_0 = run(rest_kernel, (own_keys, own_keys), message_shape(4, rows, 1))
    rest_0 = hop(rest_0, OUTER_TO_INNER)
    far_across_0 = cross(own_keys, own_keys, FAR, 4, far_0)
    far_1 = send(own_keys, second_keys, FAR, 4)
    far_part = shifted(run(far_part_kernel, (second_keys,), part_of_keys(1)), "layer", -1)
    next_across_0 = cross(own_keys, own_keys, NEXT, 3, rest_0)
    far_2 = send(far_part, own_keys, FAR, 4)
    rest_part = shifted(run(rest_part_kernel, (second_keys,), part_of_keys(3)), "layer", -1)
    far_across_1 = cross(own_keys, second_keys, FAR, 4, far_1)
    next_1 = send(own_keys, second_keys, NEXT, 4, held=(next_across_0,))
    back_0 = back(own_keys, own_keys, far_across_0)
    far_across_2 = cross(far_part, own_keys, FAR, 4, far_2)
    next_2 = send(rest_part, own_keys, NEXT, 3)
    back_1 = back(own_keys, second_keys, far_across_1)
    near = run(near_kernel, (own_keys, second_keys, rest_part), message_shape(6, rows), (back_0,))
    near = hop(near, OUTER_TO_INNER)
    next_across_1 = cross(own_keys, second_keys, NEXT, 4, next_1)
    back_2 = back(rest_part, own_keys, far_across_2, 2)
    next_across_2 = cross(rest_part, own_keys, NEXT, 3, next_2, 2)
    _, out = write_tile(
        0, None, finish_kernel, (own_keys, next_across_0, rest_0, back_0, far_0, far_across_0)
    )
    part = jax.ShapeDtypeStruct((rows, width), jnp.float32)
    turned = (far_2, next_2, far_across_2)
    parts = run(
        partial_kernel,
        (own_keys, second_keys, rest_part, far_part, next_across_1, back_1, *turned),
        [part, part],
    )
    sums, out = write_tile(1, out, plain_tile_kernel, (*parts, near, back_2), part)
    _, out = write_tile(2, out, folded_tile_kernel, (sums, next_across_2))
    return out


def per_device(keys):
    own_keys = keys[0]
    layers = lax.axis_size("layer")
    half_span = layers // 2
    inverse = 1.0 / (own_keys.shape[0] * lax.axis_size("tok"))
    if lax.axis_size("tok") == 4 and layers == 4 and own_keys.shape[1] % (8 * HALF) == 0:
        return folded_line(own_keys, inverse)
    forward_list = [own_keys]
    for repeat in range(half_span):
        forward_list.append(shifted(forward_list[-1], "layer", -1))
    return reduce_scattered(own_keys, forward_list, inverse)


def solution(mesh):
    in_specs = (P("layer", ("groups", "tok"), None),)
    out_specs = P("layer", None, ("groups", "tok"), None)
    return jax.shard_map(
        per_device, mesh=mesh, in_specs=in_specs, out_specs=out_specs, check_vma=False
    )
```
